32 devices in a mesh: groups: 2 (over x), ctx: 16 (over z, y, core).
Axes of the slice: x: 2, y: 2, z: 4, core: 2. Of those that a mesh axis runs over, the one named last changes fastest.
Arguments:
- hidden_in: bfloat16 [4096, 2048], P(('groups', 'ctx')), parts along dimension 0, may hold values from -6 to 6
- queries: bfloat16 [4096, 2048], P(('groups', 'ctx')), parts along dimension 0, may hold values from -48 to 48
- keys: bfloat16 [4096, 128], P(('groups', 'ctx')), parts along dimension 0, may hold values from -8 to 8
- values: bfloat16 [4096, 128], P(('groups', 'ctx')), parts along dimension 0, may hold values from -16 to 16
- norm_gain: bfloat16 [2048], replicated, may hold values from 0.25 to 1.75
- router: bfloat16 [2048, 16], replicated, may hold values from -0.125 to 0.125
- w_gate: bfloat16 [16, 2048, 768], P('ctx'), may hold values from -0.125 to 0.125
- w_up: bfloat16 [16, 2048, 768], P('ctx'), may hold values from -0.125 to 0.125
- w_down: bfloat16 [16, 768, 2048], P('ctx'), may hold values from -0.21875 to 0.21875
- expert_ids: int32 [4096, 4], P(('groups', 'ctx')), parts along dimension 0, may hold values from 0 to 15, all different within a row; in each aligned block of 128 rows (0 to 127, 128 to 255, ...) at most 64 rows name the same one
Outputs:
- layer_out: bfloat16 [4096, 2048], P(('groups', 'ctx')), parts along dimension 0
The draws below stay inside these ranges and needn't reach their ends.
There are 2 independent parts, one for each index of `groups`. The reference program is written for one: setup_inputs(seed, part) draws one part's arguments, and reference() takes and returns one part's arrays. A program takes and returns all parts, laid end to end along the dimension named above; an argument that names none is the same for every part. Nothing has to cross between parts.
Inputs may be any that keep to these rules, and one draw needn't show every extreme that they name: `expert_ids`: each row names 4 different experts. Within the rows of one device (aligned blocks of 128 rows) no expert is named more than 64 times, a bound that some block reaches.
All inputs are finite; a program needn't handle non-finite values.
Results may differ from the reference program's by a relative error of at most 0.006.
Values may be sent and summed in bfloat16 or wider, within the bound.
No kernel may reach another device: no remote copies, remote signals or barrier semaphores. Data moves between devices by JAX's collectives and lax.ppermute only.
A program may use at most 128 MiB of HBM per device.

```python
import math
import jax
import jax.numpy as jnp
import numpy as np
from jax import lax

D = 2048
Q_HEADS = 32
KV_HEADS = 2
HEAD_DIM = 64
FF = 768
TOP = 4
TOK_DEV = 128
TOKENS = 2048
EXPERTS = 16
CAP = 64
N_CTX = 16


def draw_queries(key, part):
    key = jax.random.fold_in(key, 1)
    drawn = jnp.clip(jax.random.normal(key, (TOKENS, Q_HEADS * HEAD_DIM), jnp.float32), -6.0, 6.0)
    return drawn.astype(jnp.bfloat16)


def draw_keys(key, part):
    key = jax.random.fold_in(key, 2)
    drawn = jnp.clip(jax.random.normal(key, (TOKENS, KV_HEADS * HEAD_DIM), jnp.float32), -6.0, 6.0)
    return drawn.astype(jnp.bfloat16)


def block_scale(rng, extent, shards, smallest, high):
    gain = 1.0
    for position, blocks in shards:
        steps = jax.random.uniform(jax.random.fold_in(jax.random.fold_in(rng, 6), position), (blocks,), jnp.float32, smallest / len(shards), high / len(shards))
        gain = gain * jnp.repeat(jnp.exp(steps), extent[position] // blocks).reshape((-1,) + (1,) * (len(extent) - 1 - position))
    return gain


def deal_out(stream_key, own, number, rows, number_of, top, most, slope):
    ranking = jax.random.permutation(stream_key, number_of)
    heavy_load, common = load_shares(number_of, rows * top, most, slope, True), load_shares(number_of, rows * top, most, slope, False)
    places = jnp.arange(number_of)

    def named(lengths, offset_by):
        used = int((lengths > 0).sum())
        fixed = max(1, used // 4)
        moved = fixed + (places - fixed + offset_by * (used - fixed)) % max(1, number_of - fixed)
        return jnp.zeros((number_of,), jnp.int32).at[ranking[jnp.where(places < fixed, places, moved)]].set(jnp.asarray(lengths, jnp.int32))

    lengths = jnp.where(number % 4 == 0, named(heavy_load, number // 4), named(common, number - number // 4 - 1))
    mixed = jax.random.permutation(jax.random.fold_in(own, 3), number_of)
    source_of, sink = mixed[0:number_of // 2 * 2:2], mixed[1:number_of // 2 * 2:2]
    margin = jnp.minimum(lengths[source_of] - 1, most - lengths[sink]) // 2
    margin = jnp.where((source_of == ranking[0]) | (sink == ranking[0]) | (lengths[sink] == 0), 0, jnp.maximum(margin, 0))
    moved = jax.random.randint(jax.random.fold_in(own, 4), (number_of // 2,), 0, 1 << 20) % (margin + 1)
    lengths = lengths.at[source_of].add(-moved).at[sink].add(moved)
    labels = jnp.searchsorted(jnp.cumsum(lengths), jnp.arange(rows * top), side="right").astype(jnp.int32)
    grid = labels.reshape(top, rows).T
    grid = grid[jax.random.permutation(jax.random.fold_in(own, 1), rows)]
    offset_by = jax.random.randint(jax.random.fold_in(own, 2), (rows, 1), 0, top)
    return jnp.take_along_axis(grid, (jnp.arange(top)[None, :] + offset_by) % top, axis=1)


def load_shares(amount, total, limit, skew, full):
    portions = [(1 << 20) // math.isqrt(standing ** skew) + 1 for standing in range(1, amount + 1)]
    largest = limit if full else min(limit, max(-(-total // amount), total * portions[0] // sum(portions)))
    least = 1 if total - largest >= amount - 1 else 0
    counts, spare = [largest] + [least] * (amount - 1), total - largest - least * (amount - 1)
    while spare > 0:
        free = [i for i in range(1, amount) if counts[i] < largest] or [i for i in range(1, amount) if counts[i] < limit]
        pool, remaining = sum([portions[i] for i in free]), spare
        for i in free:
            extra = min(limit - counts[i], max(1, remaining * portions[i] // pool), spare)
            counts[i] = counts[i] + extra
            spare = spare - extra
    return np.array(counts)


def scatter_about(rng, extent, width, most, pieces=(), kind=jnp.bfloat16):
    gain = block_scale(rng, extent, pieces, -0.22, 0.18) if pieces else 1.0
    array = jax.random.normal(rng, extent, jnp.float32) * width * gain
    return jnp.minimum(jnp.maximum(array, -most), most).astype(kind)


def setup_inputs(seed: int = 0, part: int = 0) -> dict:
    splits = jax.random.split(jax.random.key(seed), 11)
    part_keys = jax.random.split(jax.random.fold_in(splits[10], part), 11)
    hidden_in = scatter_about(part_keys[0], (TOKENS, D), 1.0, 6.0, ((0, 16),))
    queries = draw_queries(jax.random.fold_in(jax.random.fold_in(splits[10], part), 71), part)
    keys = draw_keys(jax.random.fold_in(jax.random.fold_in(splits[10], part), 71), part)
    values = scatter_about(part_keys[3], (TOKENS, KV_HEADS * HEAD_DIM), 4.0, 16.0, ((0, 16),))
    norm_gain = jnp.clip(1.0 + 0.15 * jax.random.normal(splits[4], (D,), jnp.float32), 0.25, 1.75).astype(jnp.bfloat16)
    router = scatter_about(splits[5], (D, EXPERTS), D ** -0.5, 0.125)
    w_gate = scatter_about(splits[6], (EXPERTS, D, FF), D ** -0.5, 0.125, ((0, 16),))
    w_up = scatter_about(splits[7], (EXPERTS, D, FF), D ** -0.5, 0.125, ((0, 16),))
    w_down = scatter_about(splits[8], (EXPERTS, FF, D), FF ** -0.5, 0.21875, ((0, 16),))
    expert_ids_keys = jax.random.split(jax.random.fold_in(part_keys[9], 1), TOKENS // TOK_DEV)
    expert_ids_turns = jax.random.permutation(jax.random.fold_in(part_keys[9], 3), TOKENS // TOK_DEV)
    expert_ids = jax.vmap(lambda own, number: deal_out(jax.random.fold_in(part_keys[9], 2), own, number, TOK_DEV, EXPERTS, TOP, CAP, 2))(expert_ids_keys, expert_ids_turns).reshape((TOKENS, TOP))
    return dict(hidden_in=hidden_in, queries=queries, keys=keys, values=values, norm_gain=norm_gain, router=router, w_gate=w_gate, w_up=w_up, w_down=w_down, expert_ids=expert_ids)


def attend_block(query_block, block_start, key_heads, value_heads):
    group = Q_HEADS // KV_HEADS
    rows_here = query_block.shape[0]
    query_heads = query_block.reshape(rows_here, KV_HEADS, group, HEAD_DIM).astype(jnp.float32)
    scores = jnp.einsum('qgjd,kgd->qgjk', query_heads, key_heads.astype(jnp.float32)) / math.sqrt(HEAD_DIM)
    query_pos = block_start + jnp.arange(rows_here, dtype=jnp.int32)
    key_pos = jnp.arange(TOKENS, dtype=jnp.int32)
    allowed = (key_pos[None, :] <= query_pos[:, None])[:, None, None, :]
    scores = jnp.where(allowed, scores, -1e+30)
    row_max = lax.optimization_barrier(jnp.max(scores, axis=-1, keepdims=True))
    weights = jnp.where(allowed, jnp.exp(scores - row_max), 0.0)
    row_sum = lax.optimization_barrier(jnp.sum(weights, axis=-1))
    weights_b = weights.astype(jnp.bfloat16).astype(jnp.float32)
    summed = jnp.einsum('qgjk,kgd->qgjd', weights_b, value_heads.astype(jnp.float32))
    return (summed / row_sum[..., None]).reshape(rows_here, D).astype(jnp.bfloat16)

def expert_apply(arrived, gate_mat, up_mat, down_mat):
    gate_val = jnp.dot(arrived, gate_mat, preferred_element_type=jnp.float32)
    up_val = jnp.dot(arrived, up_mat, preferred_element_type=jnp.float32)
    up_part = (jax.nn.silu(gate_val) * up_val).astype(jnp.bfloat16)
    return jnp.dot(up_part, down_mat, preferred_element_type=jnp.float32).astype(jnp.bfloat16)

def reference(hidden_in, queries, keys, values, norm_gain, router, w_gate, w_up, w_down, expert_ids):
    block_rows = math.gcd(TOKENS, 512)
    key_heads = keys.reshape(TOKENS, KV_HEADS, HEAD_DIM)
    value_heads = values.reshape(TOKENS, KV_HEADS, HEAD_DIM)
    query_blocks = queries.reshape(TOKENS // block_rows, block_rows, D)
    starts = jnp.arange(TOKENS // block_rows, dtype=jnp.int32) * block_rows
    attn = lax.map(lambda pair: attend_block(pair[0], pair[1], key_heads, value_heads), (query_blocks, starts))
    attn = attn.reshape(TOKENS, D)
    mixed = hidden_in.astype(jnp.float32) + attn.astype(jnp.float32)
    mean_sq = lax.optimization_barrier(jnp.mean(mixed * mixed, axis=-1, keepdims=True))
    normed = (mixed * lax.rsqrt(mean_sq + 1e-06) * norm_gain.astype(jnp.float32)).astype(jnp.bfloat16)
    logits = jnp.dot(normed, router, preferred_element_type=jnp.float32)
    chosen = jnp.take_along_axis(logits, expert_ids, axis=1)
    sig = jax.nn.sigmoid(chosen)
    gates = sig / lax.optimization_barrier(jnp.sum(sig, axis=-1, keepdims=True))
    flat_ids = expert_ids.reshape(-1).astype(jnp.int32)
    onehot = (flat_ids[:, None] == jnp.arange(EXPERTS, dtype=jnp.int32)[None, :]).astype(jnp.int32)
    onehot = onehot.reshape(N_CTX, TOK_DEV * TOP, EXPERTS)
    ranks = jnp.cumsum(onehot, axis=1) - onehot
    slots = lax.optimization_barrier(jnp.sum(ranks * onehot, axis=-1)).reshape(-1)
    pair_index = jnp.arange(TOKENS * TOP, dtype=jnp.int32)
    source = pair_index // (TOK_DEV * TOP)
    slot_row = source * CAP + slots
    token_of = pair_index // TOP
    buffers = jnp.zeros((EXPERTS, N_CTX * CAP, D), jnp.bfloat16)
    buffers = buffers.at[flat_ids, slot_row].set(normed[token_of])
    results = lax.map(lambda quad: expert_apply(*quad), (buffers, w_gate, w_up, w_down))
    picked = results[flat_ids, slot_row].astype(jnp.float32).reshape(TOKENS, TOP, D)
    combined = lax.optimization_barrier(jnp.sum(picked * gates[:, :, None], axis=1))
    return (mixed + combined).astype(jnp.bfloat16)
```

```python
import functools

import jax
import jax.numpy as jnp
import numpy as np
from jax import lax
from jax.experimental import pallas as pl
from jax.experimental.pallas import tpu as pltpu
from jax.sharding import PartitionSpec as P

D = 2048
HEAD_DIM = 64
KV_HEADS = 2
TOP = 4
LANES = 128
PARTS = 2
BF = jnp.bfloat16
F32 = jnp.float32
VMEM_LIMIT = 56 * 1024 * 1024


def chip_ring(chips):
    if chips == 8:
        return [0, 2, 4, 6, 7, 5, 3, 1]
    return list(range(chips))


def ring_perm(ring, step):
    chips = len(ring)
    return [
        (ring[i] * 2 + core, ring[(i + step) % chips] * 2 + core)
        for i in range(chips)
        for core in range(2)
    ]


def core_perm(chips):
    return [(i, i ^ 1) for i in range(2 * chips)]


def meta_table(ring):
    chips = len(ring)
    long, short = chips // 2, chips - 1 - chips // 2
    table = np.zeros((2 * chips, chips + 2), np.int32)
    for place, chip in enumerate(ring):
        offsets = [0] + [-s for s in range(1, long + 1)] + [s for s in range(1, short + 1)]
        earlier = [i for i, off in enumerate(offsets) if ring[(place + off) % chips] < chip]
        for core in range(2):
            row = table[chip * 2 + core]
            row[0] = core
            row[1] = len(earlier)
            row[2 : 2 + len(earlier)] = earlier
    return table


def attend_kernel(
    part, chips, experts, meta, q_ref, hid_ref, kv0, kv1, gain, router, ids,
    msg_ref, mixed_ref, kbuf, vbuf, s_scr, mx, tot, acc, attn_scr,
):
    rows = q_ref.shape[0]
    pairs = D // LANES // KV_HEADS
    core, count = meta[0], meta[1]

    def swap_halves(a):
        return jnp.concatenate([a[:, HEAD_DIM:], a[:, :HEAD_DIM]], axis=1)

    for t in range(chips):
        at = slice(t * 128, (t + 1) * 128)
        k = jnp.concatenate([kv0[at, :LANES], kv1[at, :LANES]], axis=0)
        v = jnp.concatenate([kv0[at, LANES:], kv1[at, LANES:]], axis=0)
        kbuf[0, t], kbuf[1, t] = k, swap_halves(k)
        vbuf[0, t], vbuf[1, t] = v, swap_halves(v)

    m_rows = pairs * rows
    lane = lax.broadcasted_iota(jnp.int32, (m_rows, LANES), 1)
    row_in = lax.rem(lax.broadcasted_iota(jnp.int32, (m_rows, 2 * LANES), 0), rows) + part * rows
    col = lax.broadcasted_iota(jnp.int32, (m_rows, 2 * LANES), 1)
    allowed = col <= jnp.where(col < LANES, row_in, core * (4 * LANES) - 1)

    for g in range(KV_HEADS):
        q = jnp.concatenate(
            [q_ref[:, (g * pairs + j) * LANES : (g * pairs + j + 1) * LANES] for j in range(pairs)],
            axis=0,
        )
        q = q.astype(F32) * (HEAD_DIM**-0.5)
        for par in range(2):
            sel = 0 if par == g else 1
            q_par = jnp.where((lane < HEAD_DIM) == (par == 0), q, 0.0).astype(BF)

            def score(idx):
                return lax.dot_general(
                    q_par, kbuf[sel, idx], (((1,), (1,)), ((), ())), preferred_element_type=F32
                )

            s = jnp.where(allowed, score(0), -1e30)
            s_scr[0] = s
            mx[...] = jnp.maximum(s[:, :LANES], s[:, LANES:])

            def first(t, carry):
                s = score(meta[2 + t])
                s_scr[t + 1] = s
                mx[...] = jnp.maximum(mx[...], jnp.maximum(s[:, :LANES], s[:, LANES:]))
                return carry

            lax.fori_loop(0, count, first, 0)
            row_max = jnp.max(mx[...], axis=1, keepdims=True)
            mx[...] = jnp.broadcast_to(row_max, (m_rows, LANES))

            def weigh(slot, idx):
                top = mx[...]
                p = jnp.exp(s_scr[slot] - jnp.concatenate([top, top], axis=1))
                part_sum = p[:, :LANES] + p[:, LANES:]
                part_acc = jnp.dot(p.astype(BF), vbuf[sel, idx], preferred_element_type=F32)
                return part_sum, part_acc

            tot[...], acc[...] = weigh(0, 0)

            def second(t, carry):
                part_sum, part_acc = weigh(t + 1, meta[2 + t])
                tot[...] += part_sum
                acc[...] += part_acc
                return carry

            lax.fori_loop(0, count, second, 0)
            row_sum = jnp.sum(tot[...], axis=1, keepdims=True)
            out = acc[...] / row_sum
            if par == 0:
                even = out
        out = jnp.where(lane < HEAD_DIM, even, out).astype(BF)
        for j in range(pairs):
            c = (g * pairs + j) * LANES
            attn_scr[:, c : c + LANES] = out[j * rows : (j + 1) * rows]

    mixed = hid_ref[...].astype(F32) + attn_scr[...].astype(F32)
    mixed_ref[...] = mixed
    mean_sq = jnp.mean(mixed * mixed, axis=-1, keepdims=True)
    normed = (mixed * lax.rsqrt(mean_sq + 1e-06) * gain[...].astype(F32)).astype(BF)
    msg_ref[:, :D] = normed
    logits = jnp.dot(normed, router[...], preferred_element_type=F32)
    expert = lax.broadcasted_iota(jnp.int32, (rows, LANES), 1)
    picked = expert == ids[:, 0:1]
    for k in range(1, TOP):
        picked = jnp.logical_or(picked, expert == ids[:, k : k + 1])
    sig = jnp.where(picked, 1.0 / (1.0 + jnp.exp(-logits)), 0.0)
    gates = sig / jnp.sum(sig, axis=-1, keepdims=True)
    high = gates.astype(BF).astype(F32)
    low = gates - high
    low = jnp.concatenate([low[:, HEAD_DIM:], low[:, :HEAD_DIM]], axis=1)
    msg_ref[:, D:] = jnp.where(expert < HEAD_DIM, high, low).astype(BF)


def attend(part, chips, experts, meta, queries, hidden, kv0, kv1, gain, router, ids):
    rows = queries.shape[0] // PARTS
    m_rows = D // LANES // KV_HEADS * rows
    whole = lambda a: pl.BlockSpec(a.shape, lambda i: (0,) * a.ndim)
    piece = lambda a: pl.BlockSpec((rows, a.shape[1]), lambda i: (part, 0))
    keys = 2 * kv0.shape[0]
    return pl.pallas_call(
        functools.partial(attend_kernel, part, chips, experts),
        grid=(1,),
        in_specs=[
            pl.BlockSpec(memory_space=pltpu.SMEM),
            piece(queries), piece(hidden), whole(kv0), whole(kv1), whole(gain), whole(router),
            piece(ids),
        ],
        out_specs=[
            pl.BlockSpec((rows, D + LANES), lambda i: (0, 0)),
            pl.BlockSpec((rows, D), lambda i: (0, 0)),
        ],
        out_shape=[
            jax.ShapeDtypeStruct((rows, D + LANES), BF),
            jax.ShapeDtypeStruct((rows, D), F32),
        ],
        scratch_shapes=[
            pltpu.VMEM((2, chips, 2 * LANES, LANES), BF),
            pltpu.VMEM((2, chips, 2 * LANES, LANES), BF),
            pltpu.VMEM((chips, m_rows, 2 * LANES), F32),
            pltpu.VMEM((m_rows, LANES), F32),
            pltpu.VMEM((m_rows, LANES), F32),
            pltpu.VMEM((m_rows, LANES), F32),
            pltpu.VMEM((rows, D), BF),
        ],
        compiler_params=pltpu.CompilerParams(vmem_limit_bytes=VMEM_LIMIT),
        cost_estimate=pl.CostEstimate(
            flops=4 * rows * keys * D * 4, bytes_accessed=4 * 1024 * 1024,
            transcendentals=rows * keys * 32,
        ),
        name="attend",
    )(meta, queries, hidden, kv0, kv1, gain, router, ids)


def expert_kernel(blocks, last, which, *refs):
    meta, refs = refs[0], refs[1:]
    msgs, refs = refs[:blocks], refs[blocks:]
    if last:
        prev, refs = refs[0], refs[1:]
    wg, wu, wd = refs[:3]
    outs, (x, acc) = refs[3:-2], refs[-2:]
    step, steps = pl.program_id(0), pl.num_programs(0)
    rows = msgs[0].shape[0]

    @pl.when(step == 0)
    def _():
        for b in range(blocks):
            x[b * rows : (b + 1) * rows] = msgs[b][:, :D]

    gate_val = jnp.dot(x[...], wg[0], preferred_element_type=F32)
    up_val = jnp.dot(x[...], wu[0], preferred_element_type=F32)
    up_part = (gate_val / (1.0 + jnp.exp(-gate_val)) * up_val).astype(BF)
    product = jnp.dot(up_part, wd[0], preferred_element_type=F32)

    @pl.when(step == 0)
    def _():
        acc[...] = product

    @pl.when(step > 0)
    def _():
        acc[...] += product

    @pl.when(step == steps - 1)
    def _():
        if not last:
            outs[0][...] = acc[...].astype(BF)
            return
        lane = lax.broadcasted_iota(jnp.int32, (rows, LANES), 1)
        half = lax.rem(lane, HEAD_DIM)
        for b in range(blocks):
            at = slice(b * rows, (b + 1) * rows)
            gates = msgs[b][:, D:].astype(F32)
            gate0 = jnp.sum(jnp.where(half == meta[0], gates, 0.0), axis=1, keepdims=True)
            gate1 = jnp.sum(jnp.where(half == meta[1], gates, 0.0), axis=1, keepdims=True)
            mine = acc[at].astype(BF).astype(F32)
            outs[b][...] = (gate0 * prev[at].astype(F32) + gate1 * mine).astype(BF)


def expert(meta, msgs, prev, wg, wu, wd):
    blocks, rows, last = len(msgs), msgs[0].shape[0], prev is not None
    hidden = wg.shape[2]
    tile = 256 if hidden % 256 == 0 else hidden
    m_rows = blocks * rows
    whole = lambda a: pl.BlockSpec(a.shape, lambda i: (0,) * a.ndim)
    ins = list(msgs) + ([prev] if last else [])
    if last:
        out_shape = [jax.ShapeDtypeStruct((rows, D), BF)] * blocks
    else:
        out_shape = [jax.ShapeDtypeStruct((m_rows, D), BF)]
    return pl.pallas_call(
        functools.partial(expert_kernel, blocks, last, 0),
        grid=(hidden // tile,),
        in_specs=[pl.BlockSpec(memory_space=pltpu.SMEM)]
        + [whole(a) for a in ins]
        + [
            pl.BlockSpec((1, D, tile), lambda i: (0, 0, i)),
            pl.BlockSpec((1, D, tile), lambda i: (0, 0, i)),
            pl.BlockSpec((1, tile, D), lambda i: (0, i, 0)),
        ],
        out_specs=[whole(a) for a in out_shape],
        out_shape=out_shape,
        scratch_shapes=[pltpu.VMEM((m_rows, D), BF), pltpu.VMEM((m_rows, D), F32)],
        compiler_params=pltpu.CompilerParams(vmem_limit_bytes=VMEM_LIMIT),
        cost_estimate=pl.CostEstimate(
            flops=6 * m_rows * D * hidden, bytes_accessed=6 * D * hidden, transcendentals=0
        ),
        name="experts",
    )(meta, *ins, wg, wu, wd)


def experts_of(meta, msgs, own, other):
    out = []
    for first in range(0, len(msgs), 8):
        some = msgs[first : first + 8]
        prev = expert(meta, some, None, *own)[0]
        out += expert(meta, some, prev, *other)
    return out


def add(a, b):
    return (a.astype(F32) + b.astype(F32)).astype(BF)


def spread(block, ring, sign):
    chips = len(ring)
    behind, ahead = [], []
    now = block
    for _ in range(chips // 2):
        now = lax.ppermute(now, "ctx", ring_perm(ring, sign))
        behind.append(now)
    now = block
    for _ in range(chips - 1 - chips // 2):
        now = lax.ppermute(now, "ctx", ring_perm(ring, -sign))
        ahead.append(now)
    return behind, ahead


def collect(behind, ahead, ring, sign):
    now = behind[-1]
    for term in ahead[::-1]:
        now = add(lax.ppermute(now, "ctx", ring_perm(ring, sign)), term)
    one = lax.ppermute(now, "ctx", ring_perm(ring, sign))
    now = behind[-2]
    for term in behind[:-2][::-1]:
        now = add(lax.ppermute(now, "ctx", ring_perm(ring, -sign)), term)
    two = lax.ppermute(now, "ctx", ring_perm(ring, -sign))
    return one, two


def local(hidden_in, queries, keys, values, norm_gain, router, w_gate, w_up, w_down, expert_ids):
    chips = lax.axis_size("ctx") // 2
    ring = chip_ring(chips)
    experts = router.shape[1]
    me = lax.axis_index("ctx")
    meta = jnp.asarray(meta_table(ring))[me]
    names = jnp.stack([me, me ^ 1]).astype(jnp.int32)
    router_wide = jnp.pad(router, ((0, 0), (0, LANES - experts)))
    gain = norm_gain.reshape(1, D)

    swap = core_perm(chips)
    kv = jnp.concatenate([keys, values], axis=1)
    behind, ahead = spread(kv, ring, 1)
    kv0 = jnp.concatenate([kv] + behind + ahead, axis=0)
    kv1 = lax.ppermute(kv0, "ctx", swap)
    own = (w_gate, w_up, w_down)
    other = tuple(lax.ppermute(w, "ctx", swap) for w in own)

    signs = [1, -1]
    outs = []
    sent = [
        attend(part, chips, experts, meta, queries, hidden_in, kv0, kv1, gain, router_wide, expert_ids)
        for part in range(PARTS)
    ]
    for part in range(PARTS):
        msg, mixed = sent[part]
        behind, ahead = spread(msg, ring, signs[part])
        terms = experts_of(names, [msg] + behind + ahead, own, other)
        mid = 1 + len(behind)
        one, two = collect(terms[1:mid], terms[mid:], ring, signs[part])
        total = mixed + (terms[0].astype(F32) + one.astype(F32) + two.astype(F32))
        outs.append(total.astype(BF))
    return jnp.concatenate(outs, axis=0)


def solution(mesh):
    placed = (
        P(("groups", "ctx"), None),
        P(("groups", "ctx"), None),
        P(("groups", "ctx"), None),
        P(("groups", "ctx"), None),
        P(),
        P(),
        P("ctx", None, None),
        P("ctx", None, None),
        P("ctx", None, None),
        P(("groups", "ctx"), None),
    )
    return jax.shard_map(
        local, mesh=mesh, in_specs=placed, out_specs=P(("groups", "ctx"), None), check_vma=False
    )
```

```python
import functools

import jax
import jax.numpy as jnp
import numpy as np
from jax import lax
from jax.experimental import pallas as pl
from jax.experimental.pallas import tpu as pltpu
from jax.sharding import PartitionSpec as P

D = 2048
HEAD_DIM = 64
KV_HEADS = 2
TOP = 4
LANES = 128
PARTS = 2
BF = jnp.bfloat16
F32 = jnp.float32
MIB = 1024 * 1024


def chip_ring(chips):
    if chips == 8:
        return [0, 2, 4, 6, 7, 5, 3, 1]
    return list(range(chips))


def ring_perm(ring, step):
    chips = len(ring)
    return [
        (ring[i] * 2 + core, ring[(i + step) % chips] * 2 + core)
        for i in range(chips)
        for core in range(2)
    ]


def core_perm(chips):
    return [(i, i ^ 1) for i in range(2 * chips)]


def meta_table(ring):
    chips = len(ring)
    long, short = chips // 2, chips - 1 - chips // 2
    table = np.zeros((2 * chips, chips + 2), np.int32)
    for place, chip in enumerate(ring):
        offsets = [0] + [-s for s in range(1, long + 1)] + [s for s in range(1, short + 1)]
        earlier = [i for i, off in enumerate(offsets) if ring[(place + off) % chips] < chip]
        for core in range(2):
            row = table[chip * 2 + core]
            row[0] = core
            row[1] = len(earlier)
            row[2 : 2 + len(earlier)] = earlier
    return table


def attend_kernel(
    part, chips, together, table, q_ref, hid_ref, kv0, kv1, gain, router_t, ids_t,
    msg_ref, mixed_ref, q_buf, kbuf, vbuf, s_scr, mx, tot, acc, wide,
):
    rows = mixed_ref.shape[0]
    pairs = D // LANES // KV_HEADS
    m_rows = pairs * rows
    mine = pl.ds(part * rows, rows)
    me = lax.axis_index("ctx")
    core, count = table[me, 0], table[me, 1]

    def swap_halves(a):
        return jnp.concatenate([a[:, HEAD_DIM:], a[:, :HEAD_DIM]], axis=1)

    for t in range(chips):
        at = slice(t * LANES, (t + 1) * LANES)
        k = jnp.concatenate([kv0[at, :LANES], kv1[at, :LANES]], axis=0)
        v = jnp.concatenate([kv0[at, LANES:], kv1[at, LANES:]], axis=0)
        kbuf[0, t], kbuf[1, t] = k, swap_halves(k)
        vbuf[0, t], vbuf[1, t] = v, swap_halves(v)

    lane = lax.broadcasted_iota(jnp.int32, (rows, LANES), 1)
    sets = [(0, 0), (1, 1), (0, 1), (1, 0)]
    for n, (g, par) in enumerate(sets):
        for j in range(pairs):
            c = (g * pairs + j) * LANES
            q = q_ref[mine, c : c + LANES].astype(F32) * (HEAD_DIM**-0.5)
            q = jnp.where((lane < HEAD_DIM) == (par == 0), q, 0.0).astype(BF)
            q_buf[n, j * rows : (j + 1) * rows] = q

    row_in = lax.rem(lax.broadcasted_iota(jnp.int32, (m_rows, 2 * LANES), 0), rows) + part * rows
    col = lax.broadcasted_iota(jnp.int32, (m_rows, 2 * LANES), 1)
    allowed = col <= jnp.where(col < LANES, row_in, core * (4 * LANES) - 1)

    for start in range(0, 4, together):
        group = range(start, start + together)

        def score(n, idx):
            return lax.dot_general(
                q_buf[n], kbuf[n // 2, idx], (((1,), (1,)), ((), ())), preferred_element_type=F32
            )

        for n in group:
            s = jnp.where(allowed, score(n, 0), -1e30)
            s_scr[0, n - start] = s
            mx[n - start] = jnp.maximum(s[:, :LANES], s[:, LANES:])

        def first(t, carry):
            for n in group:
                s = score(n, table[me, 2 + t])
                s_scr[t + 1, n - start] = s
                mx[n - start] = jnp.maximum(mx[n - start], jnp.maximum(s[:, :LANES], s[:, LANES:]))
            return carry

        lax.fori_loop(0, count, first, 0)
        for n in group:
            row_max = jnp.max(mx[n - start], axis=1, keepdims=True)
            mx[n - start] = jnp.broadcast_to(row_max, (m_rows, LANES))

        def weigh(n, slot, idx):
            top = mx[n - start]
            p = jnp.exp(s_scr[slot, n - start] - jnp.concatenate([top, top], axis=1))
            part_sum = p[:, :LANES] + p[:, LANES:]
            part_acc = jnp.dot(p.astype(BF), vbuf[n // 2, idx], preferred_element_type=F32)
            return part_sum, part_acc

        for n in group:
            tot[n], acc[n] = weigh(n, 0, 0)

        def second(t, carry):
            for n in group:
                part_sum, part_acc = weigh(n, t + 1, table[me, 2 + t])
                tot[n] += part_sum
                acc[n] += part_acc
            return carry

        lax.fori_loop(0, count, second, 0)

    for g, even, odd in ((0, 0, 2), (1, 3, 1)):
        for j in range(pairs):
            at = slice(j * rows, (j + 1) * rows)
            c = (g * pairs + j) * LANES
            one = acc[even, at] / jnp.sum(tot[even, at], axis=1, keepdims=True)
            two = acc[odd, at] / jnp.sum(tot[odd, at], axis=1, keepdims=True)
            attn = jnp.where(lane < HEAD_DIM, one, two).astype(BF).astype(F32)
            mixed_ref[:, c : c + LANES] = hid_ref[mine, c : c + LANES].astype(F32) + attn

    mixed = mixed_ref[...]
    mean_sq = jnp.mean(mixed * mixed, axis=-1, keepdims=True)
    wide_gain = gain[...].astype(F32).reshape(1, D)
    normed = (mixed * lax.rsqrt(mean_sq + 1e-06) * wide_gain).astype(BF)
    msg_ref[:, :D] = normed

    experts = router_t.shape[0]
    wide[...] = jnp.zeros_like(wide)
    wide[:experts] = router_t[...]
    logits = lax.dot_general(
        normed, wide[...], (((1,), (1,)), ((), ())), preferred_element_type=F32
    )
    expert = lax.broadcasted_iota(jnp.int32, (LANES, LANES), 0)
    picked = expert == ids_t[0:1, :]
    for k in range(1, TOP):
        picked = jnp.logical_or(picked, expert == ids_t[k : k + 1, :])
    picked = jnp.where(picked, 1.0, 0.0).T[part * rows : (part + 1) * rows]
    sig = jnp.where(picked > 0.0, 1.0 / (1.0 + jnp.exp(-logits)), 0.0)
    gates = sig / jnp.sum(sig, axis=-1, keepdims=True)
    high = gates.astype(BF).astype(F32)
    low = gates - high
    low = jnp.concatenate([low[:, HEAD_DIM:], low[:, :HEAD_DIM]], axis=1)
    msg_ref[:, D:] = jnp.where(lane < HEAD_DIM, high, low).astype(BF)


def attend(part, chips, table, queries, hidden, kv0, kv1, gain, router_t, ids_t):
    rows = queries.shape[0] // PARTS
    m_rows = D // LANES // KV_HEADS * rows
    together = 4 if chips <= 8 else 1
    vmem = pl.BlockSpec(memory_space=pltpu.VMEM)
    return pl.pallas_call(
        functools.partial(attend_kernel, part, chips, together),
        in_specs=[pl.BlockSpec(memory_space=pltpu.SMEM)] + [vmem] * 7,
        out_specs=[vmem, vmem],
        out_shape=[
            jax.ShapeDtypeStruct((rows, D + LANES), BF),
            jax.ShapeDtypeStruct((rows, D), F32),
        ],
        scratch_shapes=[
            pltpu.VMEM((4, m_rows, LANES), BF),
            pltpu.VMEM((2, chips, 2 * LANES, LANES), BF),
            pltpu.VMEM((2, chips, 2 * LANES, LANES), BF),
            pltpu.VMEM((chips, together, m_rows, 2 * LANES), F32),
            pltpu.VMEM((together, m_rows, LANES), F32),
            pltpu.VMEM((4, m_rows, LANES), F32),
            pltpu.VMEM((4, m_rows, LANES), F32),
            pltpu.VMEM((LANES, D), BF),
        ],
        compiler_params=pltpu.CompilerParams(vmem_limit_bytes=34 * MIB),
        cost_estimate=cost(9),
        name="attend",
    )(table, queries, hidden, kv0, kv1, gain, router_t, ids_t)


def cost(micros):
    return pl.CostEstimate(flops=int(micros * 1.15e9), bytes_accessed=1 << 20, transcendentals=0)


def expert_kernel(blocks, last, *refs):
    msgs, refs = refs[:blocks], refs[blocks:]
    if last:
        prev, refs = refs[0], refs[1:]
    wg, wu, wd = refs[:3]
    outs, x = refs[3:-1], refs[-1]
    rows = msgs[0].shape[0]
    for b in range(blocks):
        x[b * rows : (b + 1) * rows] = msgs[b][:, :D]
    gate_val = jnp.dot(x[...], wg[0], preferred_element_type=F32)
    up_val = jnp.dot(x[...], wu[0], preferred_element_type=F32)
    up_part = (gate_val / (1.0 + jnp.exp(-gate_val)) * up_val).astype(BF)
    made = jnp.dot(up_part, wd[0], preferred_element_type=F32).astype(BF)
    if not last:
        outs[0][...] = made
        return
    me = lax.axis_index("ctx")
    lane = lax.broadcasted_iota(jnp.int32, (rows, LANES), 1)
    half = lax.rem(lane, HEAD_DIM)
    for b in range(blocks):
        at = slice(b * rows, (b + 1) * rows)
        gates = msgs[b][:, D:].astype(F32)
        gate0 = jnp.sum(jnp.where(half == me, gates, 0.0), axis=1, keepdims=True)
        gate1 = jnp.sum(jnp.where(half == (me ^ 1), gates, 0.0), axis=1, keepdims=True)
        both = gate0 * prev[at].astype(F32) + gate1 * made[at].astype(F32)
        outs[b][...] = both.astype(BF)


def expert(msgs, prev, wg, wu, wd):
    blocks, rows, last = len(msgs), msgs[0].shape[0], prev is not None
    m_rows = blocks * rows
    ins = list(msgs) + ([prev] if last else [])
    if last:
        out_shape = [jax.ShapeDtypeStruct((rows, D), BF)] * blocks
    else:
        out_shape = [jax.ShapeDtypeStruct((m_rows, D), BF)]
    vmem = pl.BlockSpec(memory_space=pltpu.VMEM)
    return pl.pallas_call(
        functools.partial(expert_kernel, blocks, last),
        in_specs=[vmem] * (len(ins) + 3),
        out_specs=[vmem] * len(out_shape),
        out_shape=out_shape,
        scratch_shapes=[pltpu.VMEM((m_rows, D), BF)],
        compiler_params=pltpu.CompilerParams(vmem_limit_bytes=32 * MIB),
        cost_estimate=cost(6),
        name="experts",
    )(*ins, wg, wu, wd)


def experts_of(msgs, own, other):
    out = []
    for first in range(0, len(msgs), 8):
        some = msgs[first : first + 8]
        prev = expert(some, None, *own)[0]
        out += expert(some, prev, *other)
    return out


def add(a, b):
    return (a.astype(F32) + b.astype(F32)).astype(BF)


def spread(block, ring, sign):
    chips = len(ring)
    behind, ahead = [], []
    now = block
    for _ in range(chips // 2):
        now = lax.ppermute(now, "ctx", ring_perm(ring, sign))
        behind.append(now)
    now = block
    for _ in range(chips - 1 - chips // 2):
        now = lax.ppermute(now, "ctx", ring_perm(ring, -sign))
        ahead.append(now)
    return behind, ahead


def collect(behind, ahead, ring, sign):
    now = behind[-1]
    for term in ahead[::-1]:
        now = add(lax.ppermute(now, "ctx", ring_perm(ring, sign)), term)
    one = lax.ppermute(now, "ctx", ring_perm(ring, sign))
    now = behind[-2]
    for term in behind[:-2][::-1]:
        now = add(lax.ppermute(now, "ctx", ring_perm(ring, -sign)), term)
    two = lax.ppermute(now, "ctx", ring_perm(ring, -sign))
    return one, two


def local(hidden_in, queries, keys, values, norm_gain, router, w_gate, w_up, w_down, expert_ids):
    chips = lax.axis_size("ctx") // 2
    ring = chip_ring(chips)
    table = jnp.asarray(meta_table(ring))
    router_t = router.T
    ids_t = expert_ids.T

    swap = core_perm(chips)
    kv = jnp.concatenate([keys, values], axis=1)
    behind, ahead = spread(kv, ring, 1)
    kv0 = jnp.concatenate([kv] + behind + ahead, axis=0)
    kv1 = lax.ppermute(kv0, "ctx", swap)
    own = (w_gate, w_up, w_down)
    other = tuple(lax.ppermute(w, "ctx", swap) for w in own)

    signs = [1, -1]
    outs = []
    sent = [
        attend(part, chips, table, queries, hidden_in, kv0, kv1, norm_gain, router_t, ids_t)
        for part in range(PARTS)
    ]
    for part in range(PARTS):
        msg, mixed = sent[part]
        behind, ahead = spread(msg, ring, signs[part])
        terms = experts_of([msg] + behind + ahead, own, other)
        mid = 1 + len(behind)
        one, two = collect(terms[1:mid], terms[mid:], ring, signs[part])
        total = mixed + (terms[0].astype(F32) + one.astype(F32) + two.astype(F32))
        outs.append(total.astype(BF))
    return jnp.concatenate(outs, axis=0)


def solution(mesh):
    placed = (
        P(("groups", "ctx"), None),
        P(("groups", "ctx"), None),
        P(("groups", "ctx"), None),
        P(("groups", "ctx"), None),
        P(),
        P(),
        P("ctx", None, None),
        P("ctx", None, None),
        P("ctx", None, None),
        P(("groups", "ctx"), None),
    )
    return jax.shard_map(
        local, mesh=mesh, in_specs=placed, out_specs=P(("groups", "ctx"), None), check_vma=False
    )
```

```python
import functools

import jax
import jax.numpy as jnp
from jax import lax
from jax.experimental import pallas as pl
from jax.experimental.pallas import tpu as pltpu
from jax.sharding import PartitionSpec as P

D = 2048
HEAD_DIM = 64
KV_HEADS = 2
TOP = 4
LANES = 128
PARTS = 2
BF = jnp.bfloat16
F32 = jnp.float32
MIB = 1024 * 1024
LIGHT = pl.CostEstimate(flops=1 << 20, bytes_accessed=1 << 16, transcendentals=0)


def chip_ring(chips):
    if chips == 8:
        return [0, 2, 4, 6, 7, 5, 3, 1]
    return list(range(chips))


def ring_perm(ring, step):
    chips = len(ring)
    return [
        (ring[i] * 2 + core, ring[(i + step) % chips] * 2 + core)
        for i in range(chips)
        for core in range(2)
    ]


def core_perm(chips):
    return [(i, i ^ 1) for i in range(2 * chips)]


def place_of(chip, chips):
    if chips == 8:
        row, column = chip // 2, chip % 2
        return jnp.where(column == 0, row, chips - 1 - row)
    return chip


def block_of(chip, mine, chips):
    back = lax.rem(place_of(mine, chips) - place_of(chip, chips) + chips, chips)
    long = chips // 2
    return jnp.where(back <= long, back, long + chips - back)


SETS = [(0, 0), (1, 1), (0, 1), (1, 0)]


def prepare_rows_kernel(queries, hidden, q_sets, hid_out, q_ref, hid, sems):
    copies = [
        pltpu.make_async_copy(queries, q_ref, sems.at[0]),
        pltpu.make_async_copy(hidden, hid, sems.at[1]),
    ]
    for copy in copies:
        copy.start()
    rows = q_ref.shape[0] // PARTS
    pairs = D // LANES // KV_HEADS
    lane = lax.broadcasted_iota(jnp.int32, (rows, LANES), 1)
    copies[0].wait()
    for part in range(PARTS):
        for n, (g, par) in enumerate(SETS):
            for j in range(pairs):
                c = (g * pairs + j) * LANES
                q = q_ref[part * rows : (part + 1) * rows, c : c + LANES].astype(F32)
                q = jnp.where((lane < HEAD_DIM) == (par == 0), q * (HEAD_DIM**-0.5), 0.0)
                q_sets[part, n, j * rows : (j + 1) * rows] = q.astype(BF)
    copies[1].wait()
    hid_out[...] = hid[...]


def prepare_rows(queries, hidden):
    rows = queries.shape[0] // PARTS
    m_rows = D // LANES // KV_HEADS * rows
    vmem = pl.BlockSpec(memory_space=pltpu.VMEM)
    anywhere = pl.BlockSpec(memory_space=pl.ANY)
    return pl.pallas_call(
        prepare_rows_kernel,
        in_specs=[anywhere] * 2,
        out_specs=[vmem] * 2,
        out_shape=[
            jax.ShapeDtypeStruct((PARTS, len(SETS), m_rows, LANES), BF),
            jax.ShapeDtypeStruct(hidden.shape, BF),
        ],
        scratch_shapes=[
            pltpu.VMEM(queries.shape, BF),
            pltpu.VMEM(hidden.shape, BF),
            pltpu.SemaphoreType.DMA((2,)),
        ],
        compiler_params=pltpu.CompilerParams(vmem_limit_bytes=20 * MIB),
        cost_estimate=LIGHT,
        name="prepare_rows",
    )(queries, hidden)


def prepare_gates_kernel(gain, router_t, ids_t, gain_out, wide, named):
    gain_out[...] = gain[...].astype(F32).reshape(1, D)
    experts = router_t.shape[0]
    wide[...] = jnp.zeros_like(wide)
    wide[:experts] = router_t[...]
    expert = lax.broadcasted_iota(jnp.int32, (LANES, LANES), 0)
    picked = expert == ids_t[0:1, :]
    for k in range(1, TOP):
        picked = jnp.logical_or(picked, expert == ids_t[k : k + 1, :])
    named[...] = jnp.where(picked, 1.0, 0.0).T


def prepare_gates(gain, router_t, ids_t):
    vmem = pl.BlockSpec(memory_space=pltpu.VMEM)
    return pl.pallas_call(
        prepare_gates_kernel,
        in_specs=[vmem] * 3,
        out_specs=[vmem] * 3,
        out_shape=[
            jax.ShapeDtypeStruct((1, D), F32),
            jax.ShapeDtypeStruct((LANES, D), BF),
            jax.ShapeDtypeStruct((LANES, LANES), F32),
        ],
        compiler_params=pltpu.CompilerParams(vmem_limit_bytes=20 * MIB),
        cost_estimate=LIGHT,
        name="prepare_gates",
    )(gain, router_t, ids_t)


def attend_kernel(
    part, chips, together, q_sets, hid, gain, wide, named, kv0, kv1,
    msg_ref, mixed_ref, kbuf, vbuf, s_scr, mx, tot, acc,
):
    rows = mixed_ref.shape[0]
    pairs = D // LANES // KV_HEADS
    m_rows = pairs * rows
    mine = slice(part * rows, (part + 1) * rows)
    me = lax.axis_index("ctx")
    core, count = lax.rem(me, 2), me // 2

    def swap_halves(a):
        return jnp.concatenate([a[:, HEAD_DIM:], a[:, :HEAD_DIM]], axis=1)

    for t in range(chips):
        at = slice(t * LANES, (t + 1) * LANES)
        k = jnp.concatenate([kv0[at, :LANES], kv1[at, :LANES]], axis=0)
        v = jnp.concatenate([kv0[at, LANES:], kv1[at, LANES:]], axis=0)
        kbuf[0, t], kbuf[1, t] = k, swap_halves(k)
        vbuf[0, t], vbuf[1, t] = v, swap_halves(v)

    lane = lax.broadcasted_iota(jnp.int32, (rows, LANES), 1)
    row_in = lax.rem(lax.broadcasted_iota(jnp.int32, (m_rows, 2 * LANES), 0), rows) + part * rows
    col = lax.broadcasted_iota(jnp.int32, (m_rows, 2 * LANES), 1)
    allowed = col <= jnp.where(col < LANES, row_in, core * (4 * LANES) - 1)

    for start in range(0, len(SETS), together):
        group = range(start, start + together)

        def score(n, idx):
            return lax.dot_general(
                q_sets[part, n], kbuf[n // 2, idx], (((1,), (1,)), ((), ())),
                preferred_element_type=F32,
            )

        for n in group:
            s = jnp.where(allowed, score(n, 0), -1e30)
            s_scr[0, n - start] = s
            mx[n - start] = jnp.maximum(s[:, :LANES], s[:, LANES:])

        def first(t, carry):
            for n in group:
                s = score(n, block_of(t, count, chips))
                s_scr[t + 1, n - start] = s
                mx[n - start] = jnp.maximum(mx[n - start], jnp.maximum(s[:, :LANES], s[:, LANES:]))
            return carry

        lax.fori_loop(0, count, first, 0)
        for n in group:
            row_max = jnp.max(mx[n - start], axis=1, keepdims=True)
            mx[n - start] = jnp.broadcast_to(row_max, (m_rows, LANES))

        def weigh(n, slot, idx):
            top = mx[n - start]
            p = jnp.exp(s_scr[slot, n - start] - jnp.concatenate([top, top], axis=1))
            part_sum = p[:, :LANES] + p[:, LANES:]
            part_acc = jnp.dot(p.astype(BF), vbuf[n // 2, idx], preferred_element_type=F32)
            return part_sum, part_acc

        for n in group:
            tot[n], acc[n] = weigh(n, 0, 0)

        def second(t, carry):
            for n in group:
                part_sum, part_acc = weigh(n, t + 1, block_of(t, count, chips))
                tot[n] += part_sum
                acc[n] += part_acc
            return carry

        lax.fori_loop(0, count, second, 0)

    for g in range(KV_HEADS):
        even, odd = SETS.index((g, 0)), SETS.index((g, 1))
        for j in range(pairs):
            at = slice(j * rows, (j + 1) * rows)
            c = (g * pairs + j) * LANES
            one = acc[even, at] / jnp.sum(tot[even, at], axis=1, keepdims=True)
            two = acc[odd, at] / jnp.sum(tot[odd, at], axis=1, keepdims=True)
            attn = jnp.where(lane < HEAD_DIM, one, two).astype(BF).astype(F32)
            mixed_ref[:, c : c + LANES] = hid[mine, c : c + LANES].astype(F32) + attn

    mixed = mixed_ref[...]
    mean_sq = jnp.mean(mixed * mixed, axis=-1, keepdims=True)
    normed = (mixed * lax.rsqrt(mean_sq + 1e-06) * gain[...]).astype(BF)
    msg_ref[:, :D] = normed
    logits = lax.dot_general(
        normed, wide[...], (((1,), (1,)), ((), ())), preferred_element_type=F32
    )
    sig = jnp.where(named[mine] > 0.0, 1.0 / (1.0 + jnp.exp(-logits)), 0.0)
    gates = sig / jnp.sum(sig, axis=-1, keepdims=True)
    high = gates.astype(BF).astype(F32)
    low = gates - high
    low = jnp.concatenate([low[:, HEAD_DIM:], low[:, :HEAD_DIM]], axis=1)
    msg_ref[:, D:] = jnp.where(lane < HEAD_DIM, high, low).astype(BF)


def attend(part, chips, prepared, kv0, kv1):
    rows = prepared[1].shape[0] // PARTS
    m_rows = D // LANES // KV_HEADS * rows
    sets = len(SETS)
    together = sets if chips <= 8 else 1
    vmem = pl.BlockSpec(memory_space=pltpu.VMEM)
    return pl.pallas_call(
        functools.partial(attend_kernel, part, chips, together),
        in_specs=[vmem] * 7,
        out_specs=[vmem, vmem],
        out_shape=[
            jax.ShapeDtypeStruct((rows, D + LANES), BF),
            jax.ShapeDtypeStruct((rows, D), F32),
        ],
        scratch_shapes=[
            pltpu.VMEM((2, chips, 2 * LANES, LANES), BF),
            pltpu.VMEM((2, chips, 2 * LANES, LANES), BF),
            pltpu.VMEM((chips, together, m_rows, 2 * LANES), F32),
            pltpu.VMEM((together, m_rows, LANES), F32),
            pltpu.VMEM((sets, m_rows, LANES), F32),
            pltpu.VMEM((sets, m_rows, LANES), F32),
        ],
        compiler_params=pltpu.CompilerParams(vmem_limit_bytes=(25 if chips <= 8 else 36) * MIB),
        cost_estimate=pl.CostEstimate(flops=10**10, bytes_accessed=1 << 16, transcendentals=0),
        name="attend",
    )(*prepared, kv0, kv1)


def expert_kernel(blocks, last, *refs):
    msgs, refs = refs[:blocks], refs[blocks:]
    if last:
        before, refs = refs[0], refs[1:]
    wg, wu, wd = refs[:3]
    outs, x = refs[3:-1], refs[-1]
    rows = msgs[0].shape[0]
    for b in range(blocks):
        x[b * rows : (b + 1) * rows] = msgs[b][:, :D]
    gate_val = jnp.dot(x[...], wg[0], preferred_element_type=F32)
    up_val = jnp.dot(x[...], wu[0], preferred_element_type=F32)
    up_part = (gate_val / (1.0 + jnp.exp(-gate_val)) * up_val).astype(BF)
    made = jnp.dot(up_part, wd[0], preferred_element_type=F32).astype(BF)
    if not last:
        outs[0][...] = made
        return
    me = lax.axis_index("ctx")
    lane = lax.broadcasted_iota(jnp.int32, (rows, LANES), 1)
    half = lax.rem(lane, HEAD_DIM)
    for b in range(blocks):
        at = slice(b * rows, (b + 1) * rows)
        gates = msgs[b][:, D:].astype(F32)
        gate0 = jnp.sum(jnp.where(half == me, gates, 0.0), axis=1, keepdims=True)
        gate1 = jnp.sum(jnp.where(half == (me ^ 1), gates, 0.0), axis=1, keepdims=True)
        both = gate0 * before[at].astype(F32) + gate1 * made[at].astype(F32)
        outs[b][...] = both.astype(BF)


def expert(msgs, before, weights):
    blocks, rows, last = len(msgs), msgs[0].shape[0], before is not None
    vmem = pl.BlockSpec(memory_space=pltpu.VMEM)
    ins = list(msgs) + ([before] if last else []) + list(weights)
    if last:
        out_shape = [jax.ShapeDtypeStruct((rows, D), BF)] * blocks
    else:
        out_shape = [jax.ShapeDtypeStruct((blocks * rows, D), BF)]
    return pl.pallas_call(
        functools.partial(expert_kernel, blocks, last),
        in_specs=[vmem] * len(ins),
        out_specs=[vmem] * len(out_shape),
        out_shape=out_shape,
        scratch_shapes=[pltpu.VMEM((blocks * rows, D), BF)],
        compiler_params=pltpu.CompilerParams(vmem_limit_bytes=24 * MIB),
        cost_estimate=LIGHT,
        name="experts",
    )(*ins)


def add(a, b):
    return (a.astype(F32) + b.astype(F32)).astype(BF)


def spread(block, ring, sign, meanwhile):
    chips = len(ring)
    behind, ahead = [], []
    now = block
    for step in range(chips // 2):
        now = meanwhile(step, now)
        now = lax.ppermute(now, "ctx", ring_perm(ring, sign))
        behind.append(now)
    now = block
    for _ in range(chips - 1 - chips // 2):
        now = lax.ppermute(now, "ctx", ring_perm(ring, -sign))
        ahead.append(now)
    return behind, ahead


def tie(array, *others):
    return lax.optimization_barrier((array, *others))[0]


class Order:
    def __init__(self):
        self.token = []

    def tied(self, array):
        return tie(array, *self.token) if self.token else array

    def wait(self, *arrays):
        self.token = self.token[:1] + list(arrays)

    def ran(self, array):
        self.token = [array]


class Part:
    def __init__(self, order, ring, sign, own, other):
        self.order, self.ring, self.sign, self.own, self.other = order, ring, sign, own, other
        self.long = len(ring) // 2
        self.short = len(ring) - 1 - self.long
        self.blocks, self.made, self.terms = {}, {}, {}

    def send(self, block, ahead):
        sign = -self.sign if ahead else self.sign
        return lax.ppermute(self.order.tied(block), "ctx", ring_perm(self.ring, sign))

    def out(self, step, which=(-1, 1)):
        if step <= self.long and -1 in which:
            self.blocks[-step] = self.send(self.blocks[1 - step], False)
        if step <= self.short and 1 in which:
            self.blocks[step] = self.send(self.blocks[step - 1], True)

    def wait_out(self, step, which=(-1, 1)):
        self.order.wait(*[self.blocks[n * step] for n in which if n * step in self.blocks])

    def compute(self, names, which):
        msgs = [self.blocks[n] for n in names]
        msgs[0] = self.order.tied(msgs[0])
        key = tuple(names)
        if which == 0:
            self.made[key] = expert(msgs, None, self.own)[0]
            self.order.ran(self.made[key])
        else:
            self.terms.update(zip(names, expert(msgs, self.made[key], self.other)))
            self.order.ran(self.terms[names[0]])

    def back(self, step):
        if step == 1:
            self.one, self.two = self.terms[-self.long], self.terms[1 - self.long]
        else:
            if step <= self.long:
                self.one = add(self.order.tied(self.one), self.terms[self.long + 1 - step])
            if step <= self.short:
                self.two = add(self.order.tied(self.two), self.terms[step - self.long])
        if step <= self.long:
            self.one = self.send(self.one, False)
        if step <= self.short:
            self.two = self.send(self.two, True)

    def wait_back(self, step):
        self.order.wait(*([self.one] if step <= self.long else []), *([self.two] if step <= self.short else []))

    def total(self, mixed):
        both = self.terms[0].astype(F32) + self.one.astype(F32) + self.two.astype(F32)
        return (mixed + both).astype(BF)


def local(hidden_in, queries, keys, values, norm_gain, router, w_gate, w_up, w_down, expert_ids):
    chips = lax.axis_size("ctx") // 2
    ring = chip_ring(chips)
    router_t = router.T
    ids_t = expert_ids.T

    swap = core_perm(chips)
    kv = jnp.pad(keys, ((0, 0), (0, LANES))) + jnp.pad(values, ((0, 0), (LANES, 0)))
    prepared = list(prepare_rows(queries, hidden_in))

    def meanwhile(step, now):
        if step == 1:
            return tie(now, prepared[1])
        if step == 2:
            prepared.extend(prepare_gates(norm_gain, router_t, tie(ids_t, now)))
            return tie(now, prepared[2])
        return now

    behind, ahead = spread(kv, ring, 1, meanwhile)
    kv0 = jnp.concatenate([kv] + behind + ahead, axis=0)
    kv1 = lax.ppermute(kv0, "ctx", swap)
    own = (w_gate, w_up, w_down)
    other = tuple(lax.ppermute(w, "ctx", swap) for w in own)

    long = chips // 2
    order = Order()
    a = Part(order, ring, 1, own, other)
    b = Part(order, ring, -1, own, other)
    near, last = [0, -1, 1], [-long, 1 - long]
    rest = [n for n in range(2 - long, long) if n not in near]
    mids = [rest[i : i + 4] for i in range(0, len(rest), 4)]

    a.blocks[0], mixed_a = attend(0, chips, prepared, kv0, kv1)
    a.out(1)
    order.ran(a.blocks[0])
    b.blocks[0], mixed_b = attend(1, chips, [order.tied(prepared[0])] + prepared[1:], kv0, kv1)
    order.ran(b.blocks[0])
    a.wait_out(1)
    a.out(2)
    a.compute(near, 0)
    b.out(1)
    a.compute(near, 1)
    a.wait_out(2)
    a.out(3)
    b.wait_out(1)
    b.out(2)
    b.compute(near, 0)
    for step in range(4, long):
        a.wait_out(step - 1)
        a.out(step)
        b.wait_out(step - 2)
        b.out(step - 1)
    a.wait_out(long - 1, (-1,))
    a.out(long)
    for mid in mids:
        a.compute(mid, 0)
    b.wait_out(long - 2, (-1,))
    b.out(long - 1, (-1,))
    for mid in mids:
        a.compute(mid, 1)
    b.wait_out(long - 2, (1,))
    b.out(long - 1, (1,))
    b.compute(near, 1)
    b.wait_out(long - 1, (-1,))
    b.out(long)
    a.wait_out(long)
    a.compute(last, 0)
    a.compute(last, 1)
    a.back(1)
    b.wait_out(long)
    b.compute(last, 0)
    b.compute(last, 1)
    b.back(1)
    a.wait_back(1)
    a.back(2)
    for mid in mids:
        b.compute(mid, 0)
        b.compute(mid, 1)
    for step in range(2, long):
        b.wait_back(step - 1)
        b.back(step)
        a.wait_back(step)
        a.back(step + 1)
    b.wait_back(long - 1)
    b.back(long)
    return jnp.concatenate([a.total(mixed_a), b.total(mixed_b)], axis=0)


def solution(mesh):
    placed = (
        P(("groups", "ctx"), None),
        P(("groups", "ctx"), None),
        P(("groups", "ctx"), None),
        P(("groups", "ctx"), None),
        P(),
        P(),
        P("ctx", None, None),
        P("ctx", None, None),
        P("ctx", None, None),
        P(("groups", "ctx"), None),
    )
    return jax.shard_map(
        local, mesh=mesh, in_specs=placed, out_specs=P(("groups", "ctx"), None), check_vma=False
    )
```

```python
import functools

import jax
import jax.numpy as jnp
from jax import lax
from jax.experimental import pallas as pl
from jax.experimental.pallas import tpu as pltpu
from jax.sharding import PartitionSpec as P

D = 2048
HEAD_DIM = 64
KV_HEADS = 2
TOP = 4
LANES = 128
PARTS = 2
BF = jnp.bfloat16
F32 = jnp.float32
MIB = 1024 * 1024
LIGHT = pl.CostEstimate(flops=1 << 20, bytes_accessed=1 << 16, transcendentals=0)


def chip_ring(chips):
    if chips == 8:
        return [0, 2, 4, 6, 7, 5, 3, 1]
    return list(range(chips))


def ring_perm(ring, step):
    chips = len(ring)
    return [
        (ring[i] * 2 + core, ring[(i + step) % chips] * 2 + core)
        for i in range(chips)
        for core in range(2)
    ]


def core_perm(chips):
    return [(i, i ^ 1) for i in range(2 * chips)]


def place_of(chip, chips):
    if chips == 8:
        row, column = chip // 2, chip % 2
        return jnp.where(column == 0, row, chips - 1 - row)
    return chip


def block_of(chip, mine, chips):
    back = lax.rem(place_of(mine, chips) - place_of(chip, chips) + chips, chips)
    long = chips // 2
    return jnp.where(back <= long, back, long + chips - back)


SETS = [(0, 0), (1, 1), (0, 1), (1, 0)]


def prepare_rows_kernel(queries, hidden, q_sets, hid_out, q_ref, hid, sems):
    copies = [
        pltpu.make_async_copy(queries, q_ref, sems.at[0]),
        pltpu.make_async_copy(hidden, hid, sems.at[1]),
    ]
    for copy in copies:
        copy.start()
    rows = q_ref.shape[0] // PARTS
    pairs = D // LANES // KV_HEADS
    lane = lax.broadcasted_iota(jnp.int32, (rows, LANES), 1)
    copies[0].wait()
    for part in range(PARTS):
        for n, (g, par) in enumerate(SETS):
            for j in range(pairs):
                c = (g * pairs + j) * LANES
                q = q_ref[part * rows : (part + 1) * rows, c : c + LANES].astype(F32)
                q = jnp.where((lane < HEAD_DIM) == (par == 0), q * (HEAD_DIM**-0.5), 0.0)
                q_sets[part, n, j * rows : (j + 1) * rows] = q.astype(BF)
    copies[1].wait()
    hid_out[...] = hid[...]


def prepare_rows(queries, hidden):
    rows = queries.shape[0] // PARTS
    m_rows = D // LANES // KV_HEADS * rows
    vmem = pl.BlockSpec(memory_space=pltpu.VMEM)
    anywhere = pl.BlockSpec(memory_space=pl.ANY)
    return pl.pallas_call(
        prepare_rows_kernel,
        in_specs=[anywhere] * 2,
        out_specs=[vmem] * 2,
        out_shape=[
            jax.ShapeDtypeStruct((PARTS, len(SETS), m_rows, LANES), BF),
            jax.ShapeDtypeStruct(hidden.shape, BF),
        ],
        scratch_shapes=[
            pltpu.VMEM(queries.shape, BF),
            pltpu.VMEM(hidden.shape, BF),
            pltpu.SemaphoreType.DMA((2,)),
        ],
        compiler_params=pltpu.CompilerParams(vmem_limit_bytes=20 * MIB),
        cost_estimate=LIGHT,
        name="prepare_rows",
    )(queries, hidden)


def prepare_gates_kernel(gain, router_t, gain_out, wide):
    gain_out[...] = gain[...].astype(F32).reshape(1, D)
    experts = router_t.shape[0]
    wide[...] = jnp.zeros_like(wide)
    wide[:experts] = router_t[...]


def prepare_gates(gain, router_t):
    vmem = pl.BlockSpec(memory_space=pltpu.VMEM)
    return pl.pallas_call(
        prepare_gates_kernel,
        in_specs=[vmem] * 2,
        out_specs=[vmem] * 2,
        out_shape=[
            jax.ShapeDtypeStruct((1, D), F32),
            jax.ShapeDtypeStruct((LANES, D), BF),
        ],
        compiler_params=pltpu.CompilerParams(vmem_limit_bytes=20 * MIB),
        cost_estimate=LIGHT,
        name="prepare_gates",
    )(gain, router_t)


def name_kernel(chips, kv, named):
    stride = kv.shape[0] // chips
    expert = lax.broadcasted_iota(jnp.int32, (LANES, LANES), 0).astype(F32)
    for t in range(chips):
        ids = kv[t * stride + LANES : (t + 1) * stride, :LANES].astype(F32)
        picked = expert == ids[0:1]
        for k in range(1, TOP):
            picked = jnp.logical_or(picked, expert == ids[k : k + 1])
        named[t] = jnp.where(picked, 1.0, 0.0).T


def name_blocks(chips, kv):
    vmem = pl.BlockSpec(memory_space=pltpu.VMEM)
    return pl.pallas_call(
        functools.partial(name_kernel, chips),
        in_specs=[vmem],
        out_specs=vmem,
        out_shape=jax.ShapeDtypeStruct((chips, LANES, LANES), F32),
        compiler_params=pltpu.CompilerParams(vmem_limit_bytes=20 * MIB),
        cost_estimate=LIGHT,
        name="name_blocks",
    )(kv)


def attend_kernel(
    part, chips, together, q_sets, hid, gain, kv0, kv1,
    msg_ref, mixed_ref, kbuf, vbuf, s_scr, mx, acc,
):
    rows = mixed_ref.shape[0]
    pairs = D // LANES // KV_HEADS
    m_rows = pairs * rows
    mine = slice(part * rows, (part + 1) * rows)
    me = lax.axis_index("ctx")
    core, count = lax.rem(me, 2), me // 2

    def swap_halves(a):
        return jnp.concatenate([a[:, HEAD_DIM:], a[:, :HEAD_DIM]], axis=1)

    stride = kv0.shape[0] // chips
    key_lane = lax.broadcasted_iota(jnp.int32, (2 * LANES, LANES), 1)
    ones = jnp.ones((2 * LANES, LANES), BF)
    for t in range(chips):
        at = slice(t * stride, t * stride + LANES)
        k = jnp.concatenate([kv0[at, :LANES], kv1[at, :LANES]], axis=0)
        v = jnp.concatenate([kv0[at, LANES:], kv1[at, LANES:]], axis=0)
        turned = swap_halves(v)
        kbuf[0, t], kbuf[1, t] = k, swap_halves(k)
        for n, (g, par) in enumerate(SETS):
            mine_half = (key_lane < HEAD_DIM) == (par == 0)
            vbuf[n, t] = jnp.where(mine_half, v if n < 2 else turned, ones)

    lane = lax.broadcasted_iota(jnp.int32, (rows, LANES), 1)
    row_in = lax.rem(lax.broadcasted_iota(jnp.int32, (m_rows, 2 * LANES), 0), rows) + part * rows
    col = lax.broadcasted_iota(jnp.int32, (m_rows, 2 * LANES), 1)
    allowed = col <= jnp.where(col < LANES, row_in, core * (4 * LANES) - 1)

    for start in range(0, len(SETS), together):
        group = range(start, start + together)

        def score(n, idx):
            return lax.dot_general(
                q_sets[part, n], kbuf[n // 2, idx], (((1,), (1,)), ((), ())),
                preferred_element_type=F32,
            )

        for n in group:
            s = jnp.where(allowed, score(n, 0), -1e30)
            s_scr[0, n - start] = s
            mx[n - start] = jnp.maximum(s[:, :LANES], s[:, LANES:])

        def in_runs(body):
            done = 0
            for width in (4, 2, 1):
                runs = (count - done) // width
                lax.fori_loop(0, runs, functools.partial(body, width, done), 0)
                done = done + runs * width

        def first(width, done, run, carry):
            for n in group:
                best = mx[n - start]
                for w in range(width):
                    t = done + width * run + w
                    s = score(n, block_of(t, count, chips))
                    s_scr[t + 1, n - start] = s
                    best = jnp.maximum(best, jnp.maximum(s[:, :LANES], s[:, LANES:]))
                mx[n - start] = best
            return carry

        in_runs(first)
        for n in group:
            row_max = jnp.max(mx[n - start], axis=1, keepdims=True)
            mx[n - start] = jnp.broadcast_to(row_max, (m_rows, LANES))

        def weigh(n, slot, idx):
            top = mx[n - start]
            p = jnp.exp(s_scr[slot, n - start] - jnp.concatenate([top, top], axis=1))
            return jnp.dot(p.astype(BF), vbuf[n, idx], preferred_element_type=F32)

        for n in group:
            acc[n] = weigh(n, 0, 0)

        def second(width, done, run, carry):
            for n in group:
                part_acc = 0.0
                for w in range(width):
                    t = done + width * run + w
                    part_acc = part_acc + weigh(n, t + 1, block_of(t, count, chips))
                acc[n] += part_acc
            return carry

        in_runs(second)

    for g in range(KV_HEADS):
        even, odd = SETS.index((g, 0)), SETS.index((g, 1))
        for j in range(pairs):
            at = slice(j * rows, (j + 1) * rows)
            c = (g * pairs + j) * LANES
            made = jnp.where(lane < HEAD_DIM, acc[even, at], acc[odd, at])
            sums = swap_halves(jnp.where(lane < HEAD_DIM, acc[odd, at], acc[even, at]))
            attn = (made / sums).astype(BF).astype(F32)
            mixed_ref[:, c : c + LANES] = hid[mine, c : c + LANES].astype(F32) + attn

    mixed = mixed_ref[...]
    mean_sq = jnp.mean(mixed * mixed, axis=-1, keepdims=True)
    normed = (mixed * lax.rsqrt(mean_sq + 1e-06) * gain[...]).astype(BF)
    msg_ref[...] = normed


def attend(part, chips, prepared, kv0, kv1):
    rows = prepared[1].shape[0] // PARTS
    m_rows = D // LANES // KV_HEADS * rows
    sets = len(SETS)
    together = sets if chips <= 8 else 1
    vmem = pl.BlockSpec(memory_space=pltpu.VMEM)
    return pl.pallas_call(
        functools.partial(attend_kernel, part, chips, together),
        in_specs=[vmem] * 5,
        out_specs=[vmem, vmem],
        out_shape=[
            jax.ShapeDtypeStruct((rows, D), BF),
            jax.ShapeDtypeStruct((rows, D), F32),
        ],
        scratch_shapes=[
            pltpu.VMEM((2, chips, 2 * LANES, LANES), BF),
            pltpu.VMEM((sets, chips, 2 * LANES, LANES), BF),
            pltpu.VMEM((chips, together, m_rows, 2 * LANES), F32),
            pltpu.VMEM((together, m_rows, LANES), F32),
            pltpu.VMEM((sets, m_rows, LANES), F32),
        ],
        compiler_params=pltpu.CompilerParams(vmem_limit_bytes=(25 if chips <= 8 else 36) * MIB),
        cost_estimate=pl.CostEstimate(flops=10**10, bytes_accessed=1 << 16, transcendentals=0),
        name="attend",
    )(*prepared, kv0, kv1)


def expert_kernel(blocks, mode, places, begin, *refs):
    msgs, refs = refs[:blocks], refs[blocks:]
    if mode == 1:
        before, refs = refs[0], refs[1:]
    if mode > 0:
        (wide, named), refs = refs[:2], refs[2:]
    weights, refs = refs[: 6 if mode == 2 else 3], refs[6 if mode == 2 else 3 :]
    outs, x = refs[:-1], refs[-1]
    rows = msgs[0].shape[0]
    for b in range(blocks):
        x[b * rows : (b + 1) * rows] = msgs[b][...]
    made = []
    for wg, wu, wd in zip(weights[::3], weights[1::3], weights[2::3]):
        gate_val = jnp.dot(x[...], wg[0], preferred_element_type=F32)
        up_val = jnp.dot(x[...], wu[0], preferred_element_type=F32)
        up_part = (gate_val / (1.0 + jnp.exp(-gate_val)) * up_val).astype(BF)
        made.append(jnp.dot(up_part, wd[0], preferred_element_type=F32).astype(BF))
    if mode == 0:
        outs[0][...] = made[0]
        return
    first, second = (before, made[0]) if mode == 1 else made
    me = lax.axis_index("ctx")
    logits = lax.dot_general(
        x[...], wide[...], (((1,), (1,)), ((), ())), preferred_element_type=F32
    )
    lane = lax.broadcasted_iota(jnp.int32, (rows, LANES), 1)
    for b in range(blocks):
        at = slice(b * rows, (b + 1) * rows)
        picked = named[places[b], begin : begin + rows] > 0.0
        sig = jnp.where(picked, 1.0 / (1.0 + jnp.exp(-logits[at])), 0.0)
        gates = sig / jnp.sum(sig, axis=-1, keepdims=True)
        gate0 = jnp.sum(jnp.where(lane == me, gates, 0.0), axis=1, keepdims=True)
        gate1 = jnp.sum(jnp.where(lane == (me ^ 1), gates, 0.0), axis=1, keepdims=True)
        both = gate0 * first[at].astype(F32) + gate1 * second[at].astype(F32)
        outs[b][...] = both.astype(BF)


def expert(msgs, mode, rest, weights, places=None, begin=0):
    blocks, rows = len(msgs), msgs[0].shape[0]
    vmem = pl.BlockSpec(memory_space=pltpu.VMEM)
    ins = list(msgs) + list(rest) + list(weights)
    if mode:
        out_shape = [jax.ShapeDtypeStruct((rows, D), BF)] * blocks
    else:
        out_shape = [jax.ShapeDtypeStruct((blocks * rows, D), BF)]
    return pl.pallas_call(
        functools.partial(expert_kernel, blocks, mode, places, begin),
        in_specs=[vmem] * len(ins),
        out_specs=[vmem] * len(out_shape),
        out_shape=out_shape,
        scratch_shapes=[pltpu.VMEM((blocks * rows, D), BF)],
        compiler_params=pltpu.CompilerParams(vmem_limit_bytes=24 * MIB),
        cost_estimate=pl.CostEstimate(
            flops=int((0.9 + 0.4 * blocks) * (2 if mode == 2 else 1) * 1.15e9),
            bytes_accessed=1 << 16,
            transcendentals=0,
        ),
        name="experts",
    )(*ins)


def add(a, b):
    return (a.astype(F32) + b.astype(F32)).astype(BF)


def spread(block, ring, sign, meanwhile):
    chips = len(ring)
    behind, ahead = [], []
    far = lax.ppermute(block, "ctx", ring_perm(ring, sign * (chips // 2)))
    now = block
    for step in range(chips // 2 - 1):
        now = meanwhile(step, now)
        now = lax.ppermute(now, "ctx", ring_perm(ring, sign))
        behind.append(now)
    behind.append(far)
    now = block
    for _ in range(chips - 1 - chips // 2):
        now = lax.ppermute(now, "ctx", ring_perm(ring, -sign))
        ahead.append(now)
    return behind, ahead


def tie(array, *others):
    return lax.optimization_barrier((array, *others))[0]


class Order:
    def __init__(self):
        self.token = []

    def tied(self, array):
        return tie(array, *self.token) if self.token else array

    def wait(self, *arrays):
        self.token = self.token[:1] + list(arrays)

    def ran(self, array):
        self.token = [array]


class Part:
    def __init__(self, order, ring, sign, begin, own, other):
        self.order, self.ring, self.sign, self.own, self.other = order, ring, sign, own, other
        self.begin = begin
        self.long = len(ring) // 2
        self.short = len(ring) - 1 - self.long
        self.blocks, self.made, self.terms = {}, {}, {}

    def send(self, block, ahead):
        sign = -self.sign if ahead else self.sign
        return lax.ppermute(self.order.tied(block), "ctx", ring_perm(self.ring, sign))

    def out(self, step, which=(-1, 1)):
        if step <= self.long and -1 in which:
            self.blocks[-step] = self.send(self.blocks[1 - step], False)
        if step <= self.short and 1 in which:
            self.blocks[step] = self.send(self.blocks[step - 1], True)

    def wait_out(self, step, which=(-1, 1)):
        self.order.wait(*[self.blocks[n * step] for n in which if n * step in self.blocks])

    def place(self, name):
        offset = self.sign * name
        if abs(offset) == self.long:
            return self.long
        return -offset if offset <= 0 else self.long + offset

    def compute(self, names, mode):
        msgs = [self.blocks[n] for n in names]
        msgs[0] = self.order.tied(msgs[0])
        key = tuple(names)
        if mode == 0:
            self.made[key] = expert(msgs, 0, (), self.own)[0]
            self.order.ran(self.made[key])
            return
        rest = self.gating if mode == 2 else (self.made[key],) + self.gating
        weights = self.own + self.other if mode == 2 else self.other
        places = tuple(self.place(n) for n in names)
        self.terms.update(zip(names, expert(msgs, mode, rest, weights, places, self.begin)))
        self.order.ran(self.terms[names[0]])

    def back(self, step):
        if step == 1:
            self.one, self.two = self.terms[-self.long], self.terms[1 - self.long]
        else:
            if step <= self.long:
                self.one = add(self.order.tied(self.one), self.terms[self.long + 1 - step])
            if step <= self.short:
                self.two = add(self.order.tied(self.two), self.terms[step - self.long])
        if step <= self.long:
            self.one = self.send(self.one, False)
        if step <= self.short:
            self.two = self.send(self.two, True)

    def wait_back(self, step):
        self.order.wait(*([self.one] if step <= self.long else []), *([self.two] if step <= self.short else []))

    def total(self, mixed):
        both = self.terms[0].astype(F32) + self.one.astype(F32) + self.two.astype(F32)
        return (mixed + both).astype(BF)


def local(hidden_in, queries, keys, values, norm_gain, router, w_gate, w_up, w_down, expert_ids):
    chips = lax.axis_size("ctx") // 2
    ring = chip_ring(chips)
    router_t = router.T
    ids_t = expert_ids.T
    rows = queries.shape[0]

    swap = core_perm(chips)
    kv = (
        jnp.pad(keys, ((0, 16), (0, LANES)))
        + jnp.pad(values, ((0, 16), (LANES, 0)))
        + jnp.pad(ids_t.astype(BF), ((rows, 16 - TOP), (0, LANES)))
    )
    prepared = list(prepare_rows(queries, hidden_in))

    def meanwhile(step, now):
        if step == 1:
            return tie(now, prepared[1])
        if step == 2:
            prepared.extend(prepare_gates(norm_gain, tie(router_t, prepared[1])))
            return tie(now, prepared[2])
        return now

    behind, ahead = spread(kv, ring, 1, meanwhile)
    behind[-2], behind[-1], ahead[-1] = lax.optimization_barrier(
        (behind[-2], behind[-1], ahead[-1])
    )
    kv0 = jnp.concatenate([kv] + behind + ahead, axis=0)
    kv1 = lax.ppermute(kv0, "ctx", swap)
    own = (w_gate, w_up, w_down)
    other = tuple(lax.ppermute(w, "ctx", swap) for w in own)

    long = chips // 2
    order = Order()
    half = rows // PARTS
    a = Part(order, ring, 1, 0, own, other)
    b = Part(order, ring, -1, half, own, other)
    *prepared, wide = prepared
    near, last_a, last_b = [0, -1, 1], [-long, 1 - long], [-long, 1 - long, long - 1]
    rest = [n for n in range(2 - long, long) if n not in near]
    mids_a = [rest[i : i + 4] for i in range(0, len(rest), 4)]
    rest = [n for n in rest if n not in last_b]
    mids_b = [rest[i : i + 4] for i in range(0, len(rest), 4)]

    a.blocks[0], mixed_a = attend(0, chips, prepared, kv0, kv1)
    a.out(1)
    order.ran(a.blocks[0])
    b.blocks[0], mixed_b = attend(1, chips, [order.tied(prepared[0])] + prepared[1:], kv0, kv1)
    order.ran(b.blocks[0])
    a.wait_out(1)
    a.out(2)
    named = name_blocks(chips, order.tied(kv0))
    order.ran(named)
    a.gating = b.gating = (wide, named)
    a.compute(near, 0)
    b.out(1)
    a.compute(near, 1)
    a.wait_out(2)
    a.out(3)
    b.wait_out(1)
    b.out(2)
    for step in range(4, long):
        a.wait_out(step - 1)
        a.out(step)
        b.wait_out(step - 2)
        b.out(step - 1)
    a.wait_out(long - 1, (-1,))
    a.out(long)
    for mid in mids_a:
        a.compute(mid, 0)
    b.wait_out(long - 2, (-1,))
    b.out(long - 1, (-1,))
    for mid in mids_a:
        a.compute(mid, 1)
    b.wait_out(long - 2, (1,))
    b.out(long - 1, (1,))
    b.wait_out(long - 1, (-1,))
    b.out(long)
    a.wait_out(long)
    a.compute(last_a, 2)
    b.wait_out(long - 1, (1,))
    a.back(1)
    b.wait_out(long)
    b.compute(last_b, 2)
    b.back(1)
    a.wait_back(1)
    a.back(2)
    for some in mids_b:
        b.compute(some, 2)
    b.wait_back(1)
    b.back(2)
    a.wait_back(2)
    a.back(3)
    b.compute(near, 2)
    for step in range(3, long):
        b.wait_back(step - 1)
        b.back(step)
        a.wait_back(step)
        a.back(step + 1)
    b.wait_back(long - 1)
    b.back(long)
    return jnp.concatenate([a.total(mixed_a), b.total(mixed_b)], axis=0)


def solution(mesh):
    placed = (
        P(("groups", "ctx"), None),
        P(("groups", "ctx"), None),
        P(("groups", "ctx"), None),
        P(("groups", "ctx"), None),
        P(),
        P(),
        P("ctx", None, None),
        P("ctx", None, None),
        P("ctx", None, None),
        P(("groups", "ctx"), None),
    )
    return jax.shard_map(
        local, mesh=mesh, in_specs=placed, out_specs=P(("groups", "ctx"), None), check_vma=False
    )
```

```python
import functools

import jax
import jax.numpy as jnp
from jax import lax
from jax.experimental import pallas as pl
from jax.experimental.pallas import tpu as pltpu
from jax.sharding import PartitionSpec as P

D = 2048
HEAD_DIM = 64
KV_HEADS = 2
TOP = 4
LANES = 128
PARTS = 2
BF = jnp.bfloat16
F32 = jnp.float32
MIB = 1024 * 1024
LIGHT = pl.CostEstimate(flops=1 << 20, bytes_accessed=1 << 16, transcendentals=0)


def chip_ring(chips):
    if chips == 8:
        return [0, 2, 4, 6, 7, 5, 3, 1]
    return list(range(chips))


def ring_perm(ring, step):
    chips = len(ring)
    return [
        (ring[i] * 2 + core, ring[(i + step) % chips] * 2 + core)
        for i in range(chips)
        for core in range(2)
    ]


def core_perm(chips):
    return [(i, i ^ 1) for i in range(2 * chips)]


def place_of(chip, chips):
    if chips == 8:
        row, column = chip // 2, chip % 2
        return jnp.where(column == 0, row, chips - 1 - row)
    return chip


def block_of(chip, mine, chips):
    back = lax.rem(place_of(mine, chips) - place_of(chip, chips) + chips, chips)
    long = chips // 2
    return jnp.where(back <= long, back, long + chips - back)


SETS = [(0, 0), (1, 1), (0, 1), (1, 0)]


def prepare_rows_kernel(queries, hidden, q_sets, hid_out, q_ref, hid, sems):
    copies = [
        pltpu.make_async_copy(queries, q_ref, sems.at[0]),
        pltpu.make_async_copy(hidden, hid, sems.at[1]),
    ]
    for copy in copies:
        copy.start()
    rows = q_ref.shape[0] // PARTS
    pairs = D // LANES // KV_HEADS
    lane = lax.broadcasted_iota(jnp.int32, (rows, LANES), 1)
    copies[0].wait()
    for part in range(PARTS):
        for n, (g, par) in enumerate(SETS):
            for j in range(pairs):
                c = (g * pairs + j) * LANES
                q = q_ref[part * rows : (part + 1) * rows, c : c + LANES].astype(F32)
                q = jnp.where((lane < HEAD_DIM) == (par == 0), q * (HEAD_DIM**-0.5), 0.0)
                q_sets[part, n, j * rows : (j + 1) * rows] = q.astype(BF)
    copies[1].wait()
    hid_out[...] = hid[...]


def prepare_rows(queries, hidden):
    rows = queries.shape[0] // PARTS
    m_rows = D // LANES // KV_HEADS * rows
    vmem = pl.BlockSpec(memory_space=pltpu.VMEM)
    anywhere = pl.BlockSpec(memory_space=pl.ANY)
    return pl.pallas_call(
        prepare_rows_kernel,
        in_specs=[anywhere] * 2,
        out_specs=[vmem] * 2,
        out_shape=[
            jax.ShapeDtypeStruct((PARTS, len(SETS), m_rows, LANES), BF),
            jax.ShapeDtypeStruct(hidden.shape, BF),
        ],
        scratch_shapes=[
            pltpu.VMEM(queries.shape, BF),
            pltpu.VMEM(hidden.shape, BF),
            pltpu.SemaphoreType.DMA((2,)),
        ],
        compiler_params=pltpu.CompilerParams(vmem_limit_bytes=20 * MIB),
        cost_estimate=LIGHT,
        name="prepare_rows",
    )(queries, hidden)


def prepare_gates_kernel(gain, router_t, gain_out, wide):
    gain_out[...] = gain[...].astype(F32).reshape(1, D)
    experts = router_t.shape[0]
    wide[...] = jnp.zeros_like(wide)
    wide[:experts] = router_t[...]


def prepare_gates(gain, router_t):
    vmem = pl.BlockSpec(memory_space=pltpu.VMEM)
    return pl.pallas_call(
        prepare_gates_kernel,
        in_specs=[vmem] * 2,
        out_specs=[vmem] * 2,
        out_shape=[
            jax.ShapeDtypeStruct((1, D), F32),
            jax.ShapeDtypeStruct((LANES, D), BF),
        ],
        compiler_params=pltpu.CompilerParams(vmem_limit_bytes=20 * MIB),
        cost_estimate=LIGHT,
        name="prepare_gates",
    )(gain, router_t)


def name_kernel(chips, kv, named):
    stride = kv.shape[0] // chips
    expert = lax.broadcasted_iota(jnp.int32, (LANES, LANES), 0).astype(F32)
    for t in range(chips):
        ids = kv[t * stride + LANES : (t + 1) * stride, :LANES].astype(F32)
        picked = expert == ids[0:1]
        for k in range(1, TOP):
            picked = jnp.logical_or(picked, expert == ids[k : k + 1])
        named[t] = jnp.where(picked, 1.0, 0.0).T


def name_blocks(chips, kv):
    vmem = pl.BlockSpec(memory_space=pltpu.VMEM)
    return pl.pallas_call(
        functools.partial(name_kernel, chips),
        in_specs=[vmem],
        out_specs=vmem,
        out_shape=jax.ShapeDtypeStruct((chips, LANES, LANES), F32),
        compiler_params=pltpu.CompilerParams(vmem_limit_bytes=20 * MIB),
        cost_estimate=LIGHT,
        name="name_blocks",
    )(kv)


def attend_kernel(
    part, chips, together, q_sets, hid, gain, kv0, kv1,
    msg_ref, mixed_ref, kbuf, vbuf, s_scr, mx, acc,
):
    rows = mixed_ref.shape[0]
    pairs = D // LANES // KV_HEADS
    m_rows = pairs * rows
    mine = slice(part * rows, (part + 1) * rows)
    me = lax.axis_index("ctx")
    core, count = lax.rem(me, 2), me // 2

    def swap_halves(a):
        return jnp.concatenate([a[:, HEAD_DIM:], a[:, :HEAD_DIM]], axis=1)

    stride = kv0.shape[0] // chips
    key_lane = lax.broadcasted_iota(jnp.int32, (2 * LANES, LANES), 1)
    ones = jnp.ones((2 * LANES, LANES), BF)
    for t in range(chips):
        at = slice(t * stride, t * stride + LANES)
        k = jnp.concatenate([kv0[at, :LANES], kv1[at, :LANES]], axis=0)
        v = jnp.concatenate([kv0[at, LANES:], kv1[at, LANES:]], axis=0)
        turned = swap_halves(v)
        kbuf[0, t], kbuf[1, t] = k, swap_halves(k)
        for n, (g, par) in enumerate(SETS):
            mine_half = (key_lane < HEAD_DIM) == (par == 0)
            vbuf[n, t] = jnp.where(mine_half, v if n < 2 else turned, ones)

    lane = lax.broadcasted_iota(jnp.int32, (rows, LANES), 1)
    row_in = lax.rem(lax.broadcasted_iota(jnp.int32, (m_rows, 2 * LANES), 0), rows) + part * rows
    col = lax.broadcasted_iota(jnp.int32, (m_rows, 2 * LANES), 1)
    allowed = col <= jnp.where(col < LANES, row_in, core * (4 * LANES) - 1)

    for start in range(0, len(SETS), together):
        group = range(start, start + together)

        def score(n, idx):
            return lax.dot_general(
                q_sets[part, n], kbuf[n // 2, idx], (((1,), (1,)), ((), ())),
                preferred_element_type=F32,
            )

        for n in group:
            s = jnp.where(allowed, score(n, 0), -1e30)
            s_scr[0, n - start] = s
            mx[n - start] = jnp.maximum(s[:, :LANES], s[:, LANES:])

        def in_runs(body):
            done = 0
            for width in (2, 1):
                runs = (count - done) // width
                lax.fori_loop(0, runs, functools.partial(body, width, done), 0)
                done = done + runs * width

        def first(width, done, run, carry):
            for n in group:
                best = mx[n - start]
                for w in range(width):
                    t = done + width * run + w
                    s = score(n, block_of(t, count, chips))
                    s_scr[t + 1, n - start] = s
                    best = jnp.maximum(best, jnp.maximum(s[:, :LANES], s[:, LANES:]))
                mx[n - start] = best
            return carry

        in_runs(first)
        for n in group:
            row_max = jnp.max(mx[n - start], axis=1, keepdims=True)
            mx[n - start] = jnp.broadcast_to(row_max, (m_rows, LANES))

        def weigh(n, slot, idx):
            top = mx[n - start]
            p = jnp.exp(s_scr[slot, n - start] - jnp.concatenate([top, top], axis=1))
            return jnp.dot(p.astype(BF), vbuf[n, idx], preferred_element_type=F32)

        for n in group:
            acc[n] = weigh(n, 0, 0)

        def second(width, done, run, carry):
            for n in group:
                part_acc = 0.0
                for w in range(width):
                    t = done + width * run + w
                    part_acc = part_acc + weigh(n, t + 1, block_of(t, count, chips))
                acc[n] += part_acc
            return carry

        in_runs(second)

    for g in range(KV_HEADS):
        even, odd = SETS.index((g, 0)), SETS.index((g, 1))
        for j in range(pairs):
            at = slice(j * rows, (j + 1) * rows)
            c = (g * pairs + j) * LANES
            made = jnp.where(lane < HEAD_DIM, acc[even, at], acc[odd, at])
            sums = swap_halves(jnp.where(lane < HEAD_DIM, acc[odd, at], acc[even, at]))
            attn = (made / sums).astype(BF).astype(F32)
            mixed_ref[:, c : c + LANES] = hid[mine, c : c + LANES].astype(F32) + attn

    mixed = mixed_ref[...]
    mean_sq = jnp.mean(mixed * mixed, axis=-1, keepdims=True)
    normed = (mixed * lax.rsqrt(mean_sq + 1e-06) * gain[...]).astype(BF)
    msg_ref[...] = normed


def attend(part, chips, prepared, kv0, kv1):
    rows = prepared[1].shape[0] // PARTS
    m_rows = D // LANES // KV_HEADS * rows
    sets = len(SETS)
    together = sets if chips <= 8 else 1
    vmem = pl.BlockSpec(memory_space=pltpu.VMEM)
    return pl.pallas_call(
        functools.partial(attend_kernel, part, chips, together),
        in_specs=[vmem] * 5,
        out_specs=[vmem, vmem],
        out_shape=[
            jax.ShapeDtypeStruct((rows, D), BF),
            jax.ShapeDtypeStruct((rows, D), F32),
        ],
        scratch_shapes=[
            pltpu.VMEM((2, chips, 2 * LANES, LANES), BF),
            pltpu.VMEM((sets, chips, 2 * LANES, LANES), BF),
            pltpu.VMEM((chips, together, m_rows, 2 * LANES), F32),
            pltpu.VMEM((together, m_rows, LANES), F32),
            pltpu.VMEM((sets, m_rows, LANES), F32),
        ],
        compiler_params=pltpu.CompilerParams(vmem_limit_bytes=(25 if chips <= 8 else 36) * MIB),
        cost_estimate=pl.CostEstimate(flops=10**10, bytes_accessed=1 << 16, transcendentals=0),
        name="attend",
    )(*prepared, kv0, kv1)


def expert_kernel(blocks, mode, places, begin, *refs):
    msgs, refs = refs[:blocks], refs[blocks:]
    if mode == 1:
        before, refs = refs[0], refs[1:]
    if mode > 0:
        (wide, named), refs = refs[:2], refs[2:]
    weights, refs = refs[: 6 if mode == 2 else 3], refs[6 if mode == 2 else 3 :]
    outs, x = refs[:-1], refs[-1]
    rows = msgs[0].shape[0]
    for b in range(blocks):
        x[b * rows : (b + 1) * rows] = msgs[b][...]
    made = []
    for wg, wu, wd in zip(weights[::3], weights[1::3], weights[2::3]):
        gate_val = jnp.dot(x[...], wg[0], preferred_element_type=F32)
        up_val = jnp.dot(x[...], wu[0], preferred_element_type=F32)
        up_part = (gate_val / (1.0 + jnp.exp(-gate_val)) * up_val).astype(BF)
        made.append(jnp.dot(up_part, wd[0], preferred_element_type=F32).astype(BF))
    if mode == 0:
        outs[0][...] = made[0]
        return
    first, second = (before, made[0]) if mode == 1 else made
    me = lax.axis_index("ctx")
    logits = lax.dot_general(
        x[...], wide[...], (((1,), (1,)), ((), ())), preferred_element_type=F32
    )
    lane = lax.broadcasted_iota(jnp.int32, (rows, LANES), 1)
    for b in range(blocks):
        at = slice(b * rows, (b + 1) * rows)
        picked = named[places[b], begin : begin + rows] > 0.0
        sig = jnp.where(picked, 1.0 / (1.0 + jnp.exp(-logits[at])), 0.0)
        gates = sig / jnp.sum(sig, axis=-1, keepdims=True)
        gate0 = jnp.sum(jnp.where(lane == me, gates, 0.0), axis=1, keepdims=True)
        gate1 = jnp.sum(jnp.where(lane == (me ^ 1), gates, 0.0), axis=1, keepdims=True)
        both = gate0 * first[at].astype(F32) + gate1 * second[at].astype(F32)
        outs[b][...] = both.astype(BF)


def expert(msgs, mode, rest, weights, places=None, begin=0):
    blocks, rows = len(msgs), msgs[0].shape[0]
    vmem = pl.BlockSpec(memory_space=pltpu.VMEM)
    ins = list(msgs) + list(rest) + list(weights)
    if mode:
        out_shape = [jax.ShapeDtypeStruct((rows, D), BF)] * blocks
    else:
        out_shape = [jax.ShapeDtypeStruct((blocks * rows, D), BF)]
    return pl.pallas_call(
        functools.partial(expert_kernel, blocks, mode, places, begin),
        in_specs=[vmem] * len(ins),
        out_specs=[vmem] * len(out_shape),
        out_shape=out_shape,
        scratch_shapes=[pltpu.VMEM((blocks * rows, D), BF)],
        compiler_params=pltpu.CompilerParams(vmem_limit_bytes=24 * MIB),
        cost_estimate=pl.CostEstimate(
            flops=int((0.9 + 0.4 * blocks) * (2 if mode == 2 else 1) * 1.15e9),
            bytes_accessed=1 << 16,
            transcendentals=0,
        ),
        name="experts",
    )(*ins)


def add(a, b):
    return (a.astype(F32) + b.astype(F32)).astype(BF)


def spread(block, ring, sign, meanwhile):
    chips = len(ring)
    behind, ahead = [], []
    far = lax.ppermute(block, "ctx", ring_perm(ring, sign * (chips // 2)))
    now = block
    for step in range(chips // 2 - 1):
        now = meanwhile(step, now)
        now = lax.ppermute(now, "ctx", ring_perm(ring, sign))
        behind.append(now)
    behind.append(far)
    now = block
    for _ in range(chips - 1 - chips // 2):
        now = lax.ppermute(now, "ctx", ring_perm(ring, -sign))
        ahead.append(now)
    return behind, ahead


def tie(array, *others):
    return lax.optimization_barrier((array, *others))[0]


class Order:
    def __init__(self):
        self.token = []

    def tied(self, array):
        return tie(array, *self.token) if self.token else array

    def wait(self, *arrays):
        self.token = self.token[:1] + list(arrays)

    def ran(self, array):
        self.token = [array]


class Part:
    def __init__(self, order, ring, sign, begin, own, other):
        self.order, self.ring, self.sign, self.own, self.other = order, ring, sign, own, other
        self.begin = begin
        self.long = len(ring) // 2
        self.short = len(ring) - 1 - self.long
        self.blocks, self.made, self.terms = {}, {}, {}

    def send(self, block, ahead):
        sign = -self.sign if ahead else self.sign
        return lax.ppermute(self.order.tied(block), "ctx", ring_perm(self.ring, sign))

    def out(self, step, which=(-1, 1)):
        if step <= self.long and -1 in which:
            self.blocks[-step] = self.send(self.blocks[1 - step], False)
        if step <= self.short and 1 in which:
            self.blocks[step] = self.send(self.blocks[step - 1], True)

    def wait_out(self, step, which=(-1, 1)):
        self.order.wait(*[self.blocks[n * step] for n in which if n * step in self.blocks])

    def place(self, name):
        offset = self.sign * name
        if abs(offset) == self.long:
            return self.long
        return -offset if offset <= 0 else self.long + offset

    def compute(self, names, mode):
        msgs = [self.blocks[n] for n in names]
        msgs[0] = self.order.tied(msgs[0])
        key = tuple(names)
        if mode == 0:
            self.made[key] = expert(msgs, 0, (), self.own)[0]
            self.order.ran(self.made[key])
            return
        rest = self.gating if mode == 2 else (self.made[key],) + self.gating
        weights = self.own + self.other if mode == 2 else self.other
        places = tuple(self.place(n) for n in names)
        self.terms.update(zip(names, expert(msgs, mode, rest, weights, places, self.begin)))
        self.order.ran(self.terms[names[0]])

    def back(self, step):
        if step == 1:
            self.one, self.two = self.terms[-self.long], self.terms[1 - self.long]
        else:
            if step <= self.long:
                self.one = add(self.order.tied(self.one), self.terms[self.long + 1 - step])
            if step <= self.short:
                self.two = add(self.order.tied(self.two), self.terms[step - self.long])
        if step <= self.long:
            self.one = self.send(self.one, False)
        if step <= self.short:
            self.two = self.send(self.two, True)

    def wait_back(self, step):
        self.order.wait(*([self.one] if step <= self.long else []), *([self.two] if step <= self.short else []))

    def total(self, mixed):
        both = self.terms[0].astype(F32) + self.one.astype(F32) + self.two.astype(F32)
        return (mixed + both).astype(BF)


def local(hidden_in, queries, keys, values, norm_gain, router, w_gate, w_up, w_down, expert_ids):
    chips = lax.axis_size("ctx") // 2
    ring = chip_ring(chips)
    router_t = router.T
    ids_t = expert_ids.T
    rows = queries.shape[0]

    swap = core_perm(chips)
    kv = (
        jnp.pad(keys, ((0, 16), (0, LANES)))
        + jnp.pad(values, ((0, 16), (LANES, 0)))
        + jnp.pad(ids_t.astype(BF), ((rows, 16 - TOP), (0, LANES)))
    )
    prepared = list(prepare_rows(queries, hidden_in))

    def meanwhile(step, now):
        if step == 1:
            return tie(now, prepared[1])
        if step == 2:
            prepared.extend(prepare_gates(norm_gain, tie(router_t, prepared[1])))
            return tie(now, prepared[2])
        return now

    behind, ahead = spread(kv, ring, 1, meanwhile)
    behind[-2], behind[-1], ahead[-1] = lax.optimization_barrier(
        (behind[-2], behind[-1], ahead[-1])
    )
    kv0 = jnp.concatenate([kv] + behind + ahead, axis=0)
    kv1 = lax.ppermute(kv0, "ctx", swap)
    own = (w_gate, w_up, w_down)
    other = tuple(lax.ppermute(w, "ctx", swap) for w in own)

    long = chips // 2
    order = Order()
    half = rows // PARTS
    a = Part(order, ring, 1, 0, own, other)
    b = Part(order, ring, -1, half, own, other)
    *prepared, wide = prepared
    near, last_a, last_b = [0, -1, 1], [-long, 1 - long], [-long, 1 - long, long - 1]
    rest = [n for n in range(2 - long, long) if n not in near]
    mids_a = [rest[i : i + 4] for i in range(0, len(rest), 4)]
    rest = [n for n in rest if n not in last_b]
    mids_b = [rest[i : i + 4] for i in range(0, len(rest), 4)]

    a.blocks[0], mixed_a = attend(0, chips, prepared, kv0, kv1)
    a.out(1)
    order.ran(a.blocks[0])
    b.blocks[0], mixed_b = attend(1, chips, [order.tied(prepared[0])] + prepared[1:], kv0, kv1)
    order.ran(b.blocks[0])
    a.wait_out(1)
    a.out(2)
    named = name_blocks(chips, order.tied(kv0))
    order.ran(named)
    a.gating = b.gating = (wide, named)
    a.compute(near, 0)
    b.out(1)
    a.compute(near, 1)
    a.wait_out(2)
    a.out(3)
    b.wait_out(1)
    b.out(2)
    for step in range(4, long):
        a.wait_out(step - 1)
        a.out(step)
        b.wait_out(step - 2)
        b.out(step - 1)
    a.wait_out(long - 1, (-1,))
    a.out(long)
    for mid in mids_a:
        a.compute(mid, 0)
    b.wait_out(long - 2, (-1,))
    b.out(long - 1, (-1,))
    for mid in mids_a:
        a.compute(mid, 1)
    b.wait_out(long - 2, (1,))
    b.out(long - 1, (1,))
    b.wait_out(long - 1, (-1,))
    b.out(long)
    a.wait_out(long)
    a.compute(last_a, 2)
    b.wait_out(long - 1, (1,))
    a.back(1)
    b.wait_out(long)
    b.compute(last_b, 2)
    b.back(1)
    a.wait_back(1)
    a.back(2)
    for some in mids_b:
        b.compute(some, 2)
    b.wait_back(1)
    b.back(2)
    a.wait_back(2)
    a.back(3)
    b.compute(near, 2)
    for step in range(3, long):
        b.wait_back(step - 1)
        b.back(step)
        a.wait_back(step)
        a.back(step + 1)
    b.wait_back(long - 1)
    b.back(long)
    return jnp.concatenate([a.total(mixed_a), b.total(mixed_b)], axis=0)


def solution(mesh):
    placed = (
        P(("groups", "ctx"), None),
        P(("groups", "ctx"), None),
        P(("groups", "ctx"), None),
        P(("groups", "ctx"), None),
        P(),
        P(),
        P("ctx", None, None),
        P("ctx", None, None),
        P("ctx", None, None),
        P(("groups", "ctx"), None),
    )
    return jax.shard_map(
        local, mesh=mesh, in_specs=placed, out_specs=P(("groups", "ctx"), None), check_vma=False
    )
```

```python
import functools

import jax
import jax.numpy as jnp
from jax import lax
from jax.experimental import pallas as pl
from jax.experimental.pallas import tpu as pltpu
from jax.sharding import PartitionSpec as P

D = 2048
HEAD_DIM = 64
KV_HEADS = 2
TOP = 4
LANES = 128
PARTS = 2
BF = jnp.bfloat16
F32 = jnp.float32
MIB = 1024 * 1024
LIGHT = pl.CostEstimate(flops=1 << 20, bytes_accessed=1 << 16, transcendentals=0)


def chip_ring(chips):
    if chips == 8:
        return [0, 2, 4, 6, 7, 5, 3, 1]
    return list(range(chips))


def ring_perm(ring, step):
    chips = len(ring)
    return [
        (ring[i] * 2 + core, ring[(i + step) % chips] * 2 + core)
        for i in range(chips)
        for core in range(2)
    ]


def core_perm(chips):
    return [(i, i ^ 1) for i in range(2 * chips)]


def place_of(chip, chips):
    if chips == 8:
        row, column = chip // 2, chip % 2
        return jnp.where(column == 0, row, chips - 1 - row)
    return chip


def block_of(chip, mine, chips):
    back = lax.rem(place_of(mine, chips) - place_of(chip, chips) + chips, chips)
    long = chips // 2
    return jnp.where(back <= long, back, long + chips - back)


SETS = [(0, 0), (1, 1), (0, 1), (1, 0)]


def prepare_rows_kernel(queries, hidden, q_sets, hid_out, q_ref, hid, sems):
    copies = [
        pltpu.make_async_copy(queries, q_ref, sems.at[0]),
        pltpu.make_async_copy(hidden, hid, sems.at[1]),
    ]
    for copy in copies:
        copy.start()
    rows = q_ref.shape[0] // PARTS
    pairs = D // LANES // KV_HEADS
    lane = lax.broadcasted_iota(jnp.int32, (rows, LANES), 1)
    copies[0].wait()
    for part in range(PARTS):
        for n, (g, par) in enumerate(SETS):
            for j in range(pairs):
                c = (g * pairs + j) * LANES
                q = q_ref[part * rows : (part + 1) * rows, c : c + LANES].astype(F32)
                q = jnp.where((lane < HEAD_DIM) == (par == 0), q * (HEAD_DIM**-0.5), 0.0)
                q_sets[part, n, j * rows : (j + 1) * rows] = q.astype(BF)
    copies[1].wait()
    hid_out[...] = hid[...]


def prepare_rows(queries, hidden):
    rows = queries.shape[0] // PARTS
    m_rows = D // LANES // KV_HEADS * rows
    vmem = pl.BlockSpec(memory_space=pltpu.VMEM)
    anywhere = pl.BlockSpec(memory_space=pl.ANY)
    return pl.pallas_call(
        prepare_rows_kernel,
        in_specs=[anywhere] * 2,
        out_specs=[vmem] * 2,
        out_shape=[
            jax.ShapeDtypeStruct((PARTS, len(SETS), m_rows, LANES), BF),
            jax.ShapeDtypeStruct(hidden.shape, BF),
        ],
        scratch_shapes=[
            pltpu.VMEM(queries.shape, BF),
            pltpu.VMEM(hidden.shape, BF),
            pltpu.SemaphoreType.DMA((2,)),
        ],
        compiler_params=pltpu.CompilerParams(vmem_limit_bytes=20 * MIB),
        cost_estimate=LIGHT,
        name="prepare_rows",
    )(queries, hidden)


def prepare_gates_kernel(gain, router_t, gain_out, wide):
    gain_out[...] = gain[...].astype(F32).reshape(1, D)
    experts = router_t.shape[0]
    wide[...] = jnp.zeros_like(wide)
    wide[:experts] = router_t[...]


def prepare_gates(gain, router_t):
    vmem = pl.BlockSpec(memory_space=pltpu.VMEM)
    return pl.pallas_call(
        prepare_gates_kernel,
        in_specs=[vmem] * 2,
        out_specs=[vmem] * 2,
        out_shape=[
            jax.ShapeDtypeStruct((1, D), F32),
            jax.ShapeDtypeStruct((LANES, D), BF),
        ],
        compiler_params=pltpu.CompilerParams(vmem_limit_bytes=20 * MIB),
        cost_estimate=LIGHT,
        name="prepare_gates",
    )(gain, router_t)


def name_kernel(chips, kv, named):
    stride = kv.shape[0] // chips
    expert = lax.broadcasted_iota(jnp.int32, (LANES, LANES), 0).astype(F32)
    for t in range(chips):
        ids = kv[t * stride + LANES : (t + 1) * stride, :LANES].astype(F32)
        picked = expert == ids[0:1]
        for k in range(1, TOP):
            picked = jnp.logical_or(picked, expert == ids[k : k + 1])
        named[t] = jnp.where(picked, 1.0, 0.0).T


def name_blocks(chips, kv):
    vmem = pl.BlockSpec(memory_space=pltpu.VMEM)
    return pl.pallas_call(
        functools.partial(name_kernel, chips),
        in_specs=[vmem],
        out_specs=vmem,
        out_shape=jax.ShapeDtypeStruct((chips, LANES, LANES), F32),
        compiler_params=pltpu.CompilerParams(vmem_limit_bytes=20 * MIB),
        cost_estimate=LIGHT,
        name="name_blocks",
    )(kv)


def attend_kernel(
    part, chips, together, q_sets, hid, gain, kv0, kv1,
    msg_ref, mixed_ref, kbuf, vbuf, s_scr, mx, acc,
):
    rows = mixed_ref.shape[0]
    pairs = D // LANES // KV_HEADS
    m_rows = pairs * rows
    mine = slice(part * rows, (part + 1) * rows)
    me = lax.axis_index("ctx")
    core, count = lax.rem(me, 2), me // 2

    def swap_halves(a):
        return jnp.concatenate([a[:, HEAD_DIM:], a[:, :HEAD_DIM]], axis=1)

    stride = kv0.shape[0] // chips
    key_lane = lax.broadcasted_iota(jnp.int32, (2 * LANES, LANES), 1)
    ones = jnp.ones((2 * LANES, LANES), BF)
    for t in range(chips):
        at = slice(t * stride, t * stride + LANES)
        k = jnp.concatenate([kv0[at, :LANES], kv1[at, :LANES]], axis=0)
        v = jnp.concatenate([kv0[at, LANES:], kv1[at, LANES:]], axis=0)
        turned = swap_halves(v)
        kbuf[0, t], kbuf[1, t] = k, swap_halves(k)
        for n, (g, par) in enumerate(SETS):
            mine_half = (key_lane < HEAD_DIM) == (par == 0)
            vbuf[n, t] = jnp.where(mine_half, v if n < 2 else turned, ones)

    lane = lax.broadcasted_iota(jnp.int32, (rows, LANES), 1)
    row_in = lax.rem(lax.broadcasted_iota(jnp.int32, (m_rows, 2 * LANES), 0), rows) + part * rows
    col = lax.broadcasted_iota(jnp.int32, (m_rows, 2 * LANES), 1)
    allowed = col <= jnp.where(col < LANES, row_in, core * (4 * LANES) - 1)

    for start in range(0, len(SETS), together):
        group = range(start, start + together)

        def score(n, idx):
            return lax.dot_general(
                q_sets[part, n], kbuf[n // 2, idx], (((1,), (1,)), ((), ())),
                preferred_element_type=F32,
            )

        for n in group:
            s = jnp.where(allowed, score(n, 0), -1e30)
            s_scr[0, n - start] = s
            mx[n - start] = jnp.maximum(s[:, :LANES], s[:, LANES:])

        def in_runs(body):
            done = 0
            for width in (1,):
                runs = (count - done) // width
                lax.fori_loop(0, runs, functools.partial(body, width, done), 0)
                done = done + runs * width

        def first(width, done, run, carry):
            for n in group:
                best = mx[n - start]
                for w in range(width):
                    t = done + width * run + w
                    s = score(n, block_of(t, count, chips))
                    s_scr[t + 1, n - start] = s
                    best = jnp.maximum(best, jnp.maximum(s[:, :LANES], s[:, LANES:]))
                mx[n - start] = best
            return carry

        in_runs(first)
        for n in group:
            row_max = jnp.max(mx[n - start], axis=1, keepdims=True)
            mx[n - start] = jnp.broadcast_to(row_max, (m_rows, LANES))

        def weigh(n, slot, idx):
            top = mx[n - start]
            p = jnp.exp(s_scr[slot, n - start] - jnp.concatenate([top, top], axis=1))
            return jnp.dot(p.astype(BF), vbuf[n, idx], preferred_element_type=F32)

        for n in group:
            acc[n] = weigh(n, 0, 0)

        def second(width, done, run, carry):
            for n in group:
                part_acc = 0.0
                for w in range(width):
                    t = done + width * run + w
                    part_acc = part_acc + weigh(n, t + 1, block_of(t, count, chips))
                acc[n] += part_acc
            return carry

        in_runs(second)

    for g in range(KV_HEADS):
        even, odd = SETS.index((g, 0)), SETS.index((g, 1))
        for j in range(pairs):
            at = slice(j * rows, (j + 1) * rows)
            c = (g * pairs + j) * LANES
            made = jnp.where(lane < HEAD_DIM, acc[even, at], acc[odd, at])
            sums = swap_halves(jnp.where(lane < HEAD_DIM, acc[odd, at], acc[even, at]))
            attn = (made / sums).astype(BF).astype(F32)
            mixed_ref[:, c : c + LANES] = hid[mine, c : c + LANES].astype(F32) + attn

    mixed = mixed_ref[...]
    mean_sq = jnp.mean(mixed * mixed, axis=-1, keepdims=True)
    normed = (mixed * lax.rsqrt(mean_sq + 1e-06) * gain[...]).astype(BF)
    msg_ref[...] = normed


def attend(part, chips, prepared, kv0, kv1):
    rows = prepared[1].shape[0] // PARTS
    m_rows = D // LANES // KV_HEADS * rows
    sets = len(SETS)
    together = sets if chips <= 8 else 1
    vmem = pl.BlockSpec(memory_space=pltpu.VMEM)
    return pl.pallas_call(
        functools.partial(attend_kernel, part, chips, together),
        in_specs=[vmem] * 5,
        out_specs=[vmem, vmem],
        out_shape=[
            jax.ShapeDtypeStruct((rows, D), BF),
            jax.ShapeDtypeStruct((rows, D), F32),
        ],
        scratch_shapes=[
            pltpu.VMEM((2, chips, 2 * LANES, LANES), BF),
            pltpu.VMEM((sets, chips, 2 * LANES, LANES), BF),
            pltpu.VMEM((chips, together, m_rows, 2 * LANES), F32),
            pltpu.VMEM((together, m_rows, LANES), F32),
            pltpu.VMEM((sets, m_rows, LANES), F32),
        ],
        compiler_params=pltpu.CompilerParams(vmem_limit_bytes=(25 if chips <= 8 else 36) * MIB),
        cost_estimate=pl.CostEstimate(flops=10**10, bytes_accessed=1 << 16, transcendentals=0),
        name="attend",
    )(*prepared, kv0, kv1)


def expert_kernel(blocks, mode, places, begin, *refs):
    msgs, refs = refs[:blocks], refs[blocks:]
    if mode == 1:
        before, refs = refs[0], refs[1:]
    if mode > 0:
        (wide, named), refs = refs[:2], refs[2:]
    weights, refs = refs[: 6 if mode == 2 else 3], refs[6 if mode == 2 else 3 :]
    outs, x = refs[:-1], refs[-1]
    rows = msgs[0].shape[0]
    for b in range(blocks):
        x[b * rows : (b + 1) * rows] = msgs[b][...]
    made = []
    for wg, wu, wd in zip(weights[::3], weights[1::3], weights[2::3]):
        gate_val = jnp.dot(x[...], wg[0], preferred_element_type=F32)
        up_val = jnp.dot(x[...], wu[0], preferred_element_type=F32)
        up_part = (gate_val / (1.0 + jnp.exp(-gate_val)) * up_val).astype(BF)
        made.append(jnp.dot(up_part, wd[0], preferred_element_type=F32).astype(BF))
    if mode == 0:
        outs[0][...] = made[0]
        return
    first, second = (before, made[0]) if mode == 1 else made
    me = lax.axis_index("ctx")
    logits = lax.dot_general(
        x[...], wide[...], (((1,), (1,)), ((), ())), preferred_element_type=F32
    )
    lane = lax.broadcasted_iota(jnp.int32, (rows, LANES), 1)
    for b in range(blocks):
        at = slice(b * rows, (b + 1) * rows)
        picked = named[places[b], begin : begin + rows] > 0.0
        sig = jnp.where(picked, 1.0 / (1.0 + jnp.exp(-logits[at])), 0.0)
        gates = sig / jnp.sum(sig, axis=-1, keepdims=True)
        gate0 = jnp.sum(jnp.where(lane == me, gates, 0.0), axis=1, keepdims=True)
        gate1 = jnp.sum(jnp.where(lane == (me ^ 1), gates, 0.0), axis=1, keepdims=True)
        both = gate0 * first[at].astype(F32) + gate1 * second[at].astype(F32)
        outs[b][...] = both.astype(BF)


def expert(msgs, mode, rest, weights, places=None, begin=0):
    blocks, rows = len(msgs), msgs[0].shape[0]
    vmem = pl.BlockSpec(memory_space=pltpu.VMEM)
    ins = list(msgs) + list(rest) + list(weights)
    if mode:
        out_shape = [jax.ShapeDtypeStruct((rows, D), BF)] * blocks
    else:
        out_shape = [jax.ShapeDtypeStruct((blocks * rows, D), BF)]
    return pl.pallas_call(
        functools.partial(expert_kernel, blocks, mode, places, begin),
        in_specs=[vmem] * len(ins),
        out_specs=[vmem] * len(out_shape),
        out_shape=out_shape,
        scratch_shapes=[pltpu.VMEM((blocks * rows, D), BF)],
        compiler_params=pltpu.CompilerParams(vmem_limit_bytes=24 * MIB),
        cost_estimate=pl.CostEstimate(
            flops=int((0.9 + 0.4 * blocks) * (2 if mode == 2 else 1) * 1.15e9),
            bytes_accessed=1 << 16,
            transcendentals=0,
        ),
        name="experts",
    )(*ins)


def add(a, b):
    return (a.astype(F32) + b.astype(F32)).astype(BF)


def spread(block, ring, sign, meanwhile):
    chips = len(ring)
    behind, ahead = [], []
    far = lax.ppermute(block, "ctx", ring_perm(ring, sign * (chips // 2)))
    now = block
    for step in range(chips // 2 - 1):
        now = meanwhile(step, now)
        now = lax.ppermute(now, "ctx", ring_perm(ring, sign))
        behind.append(now)
    behind.append(far)
    now = block
    for _ in range(chips - 1 - chips // 2):
        now = lax.ppermute(now, "ctx", ring_perm(ring, -sign))
        ahead.append(now)
    return behind, ahead


def tie(array, *others):
    return lax.optimization_barrier((array, *others))[0]


class Order:
    def __init__(self):
        self.token = []

    def tied(self, array):
        return tie(array, *self.token) if self.token else array

    def wait(self, *arrays):
        self.token = self.token[:1] + list(arrays)

    def ran(self, array):
        self.token = [array]


class Part:
    def __init__(self, order, ring, sign, begin, own, other):
        self.order, self.ring, self.sign, self.own, self.other = order, ring, sign, own, other
        self.begin = begin
        self.long = len(ring) // 2
        self.short = len(ring) - 1 - self.long
        self.blocks, self.made, self.terms = {}, {}, {}

    def send(self, block, ahead):
        sign = -self.sign if ahead else self.sign
        return lax.ppermute(self.order.tied(block), "ctx", ring_perm(self.ring, sign))

    def out(self, step, which=(-1, 1)):
        if step <= self.long and -1 in which:
            self.blocks[-step] = self.send(self.blocks[1 - step], False)
        if step <= self.short and 1 in which:
            self.blocks[step] = self.send(self.blocks[step - 1], True)

    def wait_out(self, step, which=(-1, 1)):
        self.order.wait(*[self.blocks[n * step] for n in which if n * step in self.blocks])

    def place(self, name):
        offset = self.sign * name
        if abs(offset) == self.long:
            return self.long
        return -offset if offset <= 0 else self.long + offset

    def compute(self, names, mode):
        msgs = [self.blocks[n] for n in names]
        msgs[0] = self.order.tied(msgs[0])
        key = tuple(names)
        if mode == 0:
            self.made[key] = expert(msgs, 0, (), self.own)[0]
            self.order.ran(self.made[key])
            return
        rest = self.gating if mode == 2 else (self.made[key],) + self.gating
        weights = self.own + self.other if mode == 2 else self.other
        places = tuple(self.place(n) for n in names)
        self.terms.update(zip(names, expert(msgs, mode, rest, weights, places, self.begin)))
        self.order.ran(self.terms[names[0]])

    def back(self, step):
        if step == 1:
            self.one, self.two = self.terms[-self.long], self.terms[1 - self.long]
        else:
            if step <= self.long:
                self.one = add(self.order.tied(self.one), self.terms[self.long + 1 - step])
            if step <= self.short:
                self.two = add(self.order.tied(self.two), self.terms[step - self.long])
        if step <= self.long:
            self.one = self.send(self.one, False)
        if step <= self.short:
            self.two = self.send(self.two, True)

    def wait_back(self, step):
        self.order.wait(*([self.one] if step <= self.long else []), *([self.two] if step <= self.short else []))

    def total(self, mixed):
        both = self.terms[0].astype(F32) + self.one.astype(F32) + self.two.astype(F32)
        return (mixed + both).astype(BF)


def local(hidden_in, queries, keys, values, norm_gain, router, w_gate, w_up, w_down, expert_ids):
    chips = lax.axis_size("ctx") // 2
    ring = chip_ring(chips)
    router_t = router.T
    ids_t = expert_ids.T
    rows = queries.shape[0]

    swap = core_perm(chips)
    kv = (
        jnp.pad(keys, ((0, 16), (0, LANES)))
        + jnp.pad(values, ((0, 16), (LANES, 0)))
        + jnp.pad(ids_t.astype(BF), ((rows, 16 - TOP), (0, LANES)))
    )
    prepared = list(prepare_rows(queries, hidden_in))

    def meanwhile(step, now):
        if step == 1:
            return tie(now, prepared[1])
        if step == 2:
            prepared.extend(prepare_gates(norm_gain, tie(router_t, prepared[1])))
            return tie(now, prepared[2])
        return now

    behind, ahead = spread(kv, ring, 1, meanwhile)
    behind[-2], behind[-1], ahead[-1] = lax.optimization_barrier(
        (behind[-2], behind[-1], ahead[-1])
    )
    kv0 = jnp.concatenate([kv] + behind + ahead, axis=0)
    kv1 = lax.ppermute(kv0, "ctx", swap)
    own = (w_gate, w_up, w_down)
    other = tuple(lax.ppermute(w, "ctx", swap) for w in own)

    long = chips // 2
    order = Order()
    half = rows // PARTS
    a = Part(order, ring, 1, 0, own, other)
    b = Part(order, ring, -1, half, own, other)
    *prepared, wide = prepared
    near, last_a, last_b = [0, -1, 1], [-long, 1 - long], [-long, 1 - long, long - 1]
    rest = [n for n in range(2 - long, long) if n not in near]
    mids_a = [rest[i : i + 4] for i in range(0, len(rest), 4)]
    rest = [n for n in rest if n not in last_b]
    mids_b = [rest[i : i + 4] for i in range(0, len(rest), 4)]

    a.blocks[0], mixed_a = attend(0, chips, prepared, kv0, kv1)
    a.out(1)
    order.ran(a.blocks[0])
    b.blocks[0], mixed_b = attend(1, chips, [order.tied(prepared[0])] + prepared[1:], kv0, kv1)
    order.ran(b.blocks[0])
    a.wait_out(1)
    a.out(2)
    named = name_blocks(chips, order.tied(kv0))
    order.ran(named)
    a.gating = b.gating = (wide, named)
    a.compute(near, 0)
    b.out(1)
    a.compute(near, 1)
    a.wait_out(2)
    a.out(3)
    b.wait_out(1)
    b.out(2)
    for step in range(4, long):
        a.wait_out(step - 1)
        a.out(step)
        b.wait_out(step - 2)
        b.out(step - 1)
    a.wait_out(long - 1, (-1,))
    a.out(long)
    for mid in mids_a:
        a.compute(mid, 0)
    b.wait_out(long - 2, (-1,))
    b.out(long - 1, (-1,))
    for mid in mids_a:
        a.compute(mid, 1)
    b.wait_out(long - 2, (1,))
    b.out(long - 1, (1,))
    b.wait_out(long - 1, (-1,))
    b.out(long)
    a.wait_out(long)
    a.compute(last_a, 2)
    b.wait_out(long - 1, (1,))
    a.back(1)
    b.wait_out(long)
    b.compute(last_b, 2)
    b.back(1)
    a.wait_back(1)
    a.back(2)
    for some in mids_b:
        b.compute(some, 2)
    b.wait_back(1)
    b.back(2)
    a.wait_back(2)
    a.back(3)
    b.compute(near, 2)
    for step in range(3, long):
        b.wait_back(step - 1)
        b.back(step)
        a.wait_back(step)
        a.back(step + 1)
    b.wait_back(long - 1)
    b.back(long)
    return jnp.concatenate([a.total(mixed_a), b.total(mixed_b)], axis=0)


def solution(mesh):
    placed = (
        P(("groups", "ctx"), None),
        P(("groups", "ctx"), None),
        P(("groups", "ctx"), None),
        P(("groups", "ctx"), None),
        P(),
        P(),
        P("ctx", None, None),
        P("ctx", None, None),
        P("ctx", None, None),
        P(("groups", "ctx"), None),
    )
    return jax.shard_map(
        local, mesh=mesh, in_specs=placed, out_specs=P(("groups", "ctx"), None), check_vma=False
    )
```
